256 devices in a mesh: wide: 64 (over y, z, core), rep: 4 (over x).
Axes of the slice: x: 4, y: 4, z: 8, core: 2. Of those that a mesh axis runs over, the one named last changes fastest.
Arguments:
- pooled_emb: bfloat16 [2048, 39, 64], P(('wide', 'rep')), may hold values from -6 to 6
- conv_weight: float32 [14, 7], replicated, may hold values from -2 to 2
- conv_bias: float32 [14], replicated, may hold values from -3 to 3
- rec_weight: float32 [14, 19, 57], replicated, may hold values from -0.375 to 0.375
- rec_bias: float32 [57], replicated, may hold values from -3 to 3
- feat_cot: bfloat16 [2048, 96, 64], P(('wide', 'rep')), may hold values from -6 to 6
- gram_cot: bfloat16 [2048, 96, 96], P(('wide', 'rep')), may hold values from -0.59765625 to 0.59765625
- bag_ids: int32 [2048, 39, 4], P(('wide', 'rep')), may hold values from 0 to 32767, as said below
- bag_lengths: int32 [2048, 39], P(('wide', 'rep')), may hold values from 1 to 4
- field_table: int32 [39], replicated, may hold values from 0 to 25
Outputs:
- table_grad: float32 [26, 64, 32768], P(None, None, ('wide', 'rep'))
- conv_weight_grad: float32 [14, 7], replicated
- conv_bias_grad: float32 [14], replicated
- rec_weight_grad: float32 [14, 19, 57], replicated
- rec_bias_grad: float32 [57], replicated
The draws below stay inside these ranges and needn't reach their ends.
Inputs may be any that keep to these rules, and one draw needn't show every extreme that they name: `bag_ids`: each table's rows fall into 64 equal owner ranges of 512 rows. Counting live slots only, one device's samples name at most 39 rows of one owner range; one owner range receives exactly 39 from every device, and each device's other live lookups spread over the remaining owner ranges with counts that differ by at most one. Ids in slots past a bag's length are arbitrary rows.
All inputs are finite; a program needn't handle non-finite values.
Results may differ from the reference program's by a relative error of at most 0.0029.
Values may be sent and summed in bfloat16 or wider, within the bound.
A program may use at most 64 MiB of HBM per device.

```python
import math
import jax
import jax.numpy as jnp
from jax import lax

K = 64
F = 39
NT = 26
C = 14
KH = 7
BAG = 4
B_DEV = 8
T_SHARE = 128
P_SIZE = 19
NF = 57
FT = 96
SAMPLES = 2048
TROWS = 32768
CAP = 39
N_WIDE = 64
N_REP = 4


def lookup_plan(key):
    blocks = N_WIDE * N_REP
    slot_count = B_DEV * F * BAG
    key_len, key_busy, key_order, key_rot, key_off, key_pad = jax.random.split(key, 6)
    lengths = jax.random.randint(key_len, (SAMPLES, F), 1, BAG + 1).astype(jnp.int32)
    live_slot = (jnp.arange(BAG)[None, None, :] < lengths[:, :, None]).reshape(blocks, slot_count)
    slot_order = jax.vmap(lambda sub_key: jax.random.permutation(sub_key, slot_count))(jax.random.split(key_order, blocks))
    live_sorted = jnp.take_along_axis(live_slot.astype(jnp.int32), slot_order, axis=1)
    rank_sorted = jnp.cumsum(live_sorted, axis=1) - 1
    inverse = jnp.argsort(slot_order, axis=1)
    rank = jnp.take_along_axis(rank_sorted, inverse, axis=1)
    busiest = jax.random.randint(key_busy, (), 0, N_WIDE)
    rotation = jax.random.randint(key_rot, (blocks, 1), 0, N_WIDE - 1)
    others = (rank - CAP + rotation) % (N_WIDE - 1)
    others = others + (others >= busiest).astype(jnp.int32)
    owner_live = jnp.where(rank < CAP, busiest, others)
    owner_pad = jax.random.randint(key_pad, (blocks, slot_count), 0, N_WIDE)
    owner_of = jnp.where(live_slot, owner_live, owner_pad)
    offset = jax.random.randint(key_off, (blocks, slot_count), 0, N_REP * T_SHARE)
    row_ids = (owner_of * (N_REP * T_SHARE) + offset).reshape(SAMPLES, F, BAG).astype(jnp.int32)
    return (row_ids, lengths)


def draw_bag_ids(key, part):
    row_ids, lengths = lookup_plan(key)
    return row_ids


def draw_bag_lengths(key, part):
    row_ids, lengths = lookup_plan(key)
    return lengths


def set_ends(entries, key, low, largest):
    longest = entries.shape.index(max(entries.shape))
    spots = []
    for shift in (0, 1):
        where = [jax.random.randint(jax.random.fold_in(key, axis), (), 0, length) for axis, length in enumerate(entries.shape)]
        where[longest] = (where[longest] + shift) % entries.shape[longest]
        spots.append(tuple(where))
    return entries.at[spots[0]].set(low).at[spots[1]].set(largest)


def block_scale(own_key, extent, cuts, low, top_value):
    def one(axis_at, blocks):
        heights = jax.random.uniform(jax.random.fold_in(jax.random.fold_in(own_key, 6), axis_at), (blocks,), jnp.float32, low / len(cuts), top_value / len(cuts))
        return jnp.repeat(jnp.exp(heights), extent[axis_at] // blocks).reshape((-1,) + (1,) * (len(extent) - axis_at - 1))

    gain = one(*cuts[0])
    for cut in cuts[1:]:
        gain = gain * one(*cut)
    return gain


def centred(rng, extent, spread, limit, cuts=(), held_as=jnp.bfloat16):
    loudness = block_scale(rng, extent, cuts, -0.22, 0.18) if cuts else 1.0
    entries = jax.random.normal(rng, extent, jnp.float32) * spread * loudness
    return jnp.minimum(jnp.maximum(entries, -limit), limit).astype(held_as)


def setup_inputs(seed: int = 0) -> dict:
    keys = jax.random.split(jax.random.key(seed), 11)
    return {
        "pooled_emb": centred(keys[0], (SAMPLES, F, K), 1.0, 6.0, ((0, 256),)),
        "conv_weight": centred(keys[1], (C, KH), KH ** -0.5, 2.0, (), jnp.float32),
        "conv_bias": centred(keys[2], (C,), 0.5, 3.0, (), jnp.float32),
        "rec_weight": centred(keys[3], (C, P_SIZE, NF), (C * P_SIZE) ** -0.5, 0.375, (), jnp.float32),
        "rec_bias": centred(keys[4], (NF,), 0.5, 3.0, (), jnp.float32),
        "feat_cot": centred(keys[5], (SAMPLES, FT, K), 1.0, 6.0, ((0, 256),)),
        "gram_cot": centred(keys[6], (SAMPLES, FT, FT), 0.1, 0.59765625, ((0, 256),)),
        "bag_ids": draw_bag_ids(jax.random.fold_in(keys[10], 71), 0),
        "bag_lengths": draw_bag_lengths(jax.random.fold_in(keys[10], 71), 0),
        "field_table": set_ends(jax.random.randint(keys[9], (F,), 0, NT), jax.random.fold_in(keys[9], 1), 0, NT - 1).astype(jnp.int32),
    }


def dense_backward(emb_block, cot_block, gram_block, conv_weight, conv_bias, rec_weight, rec_bias):
    highest = lax.Precision.HIGHEST
    fields = emb_block.astype(jnp.float32)
    margin = (KH - 1) // 2
    padded = jnp.pad(fields, ((0, 0), (margin, margin), (0, 0)))
    shifted = jnp.stack([padded[:, shift:shift + F, :] for shift in range(KH)], axis=1)
    conv_out = jnp.einsum('cd,bdik->bcik', conv_weight, shifted, precision=highest) + conv_bias[None, :, None, None]
    activated = jnp.tanh(conv_out)
    pair_maps = activated[:, :, :2 * P_SIZE, :].reshape(activated.shape[0], C, P_SIZE, 2, K)
    pooled = 0.5 * (pair_maps[:, :, :, 0, :] + pair_maps[:, :, :, 1, :])
    recombined = jnp.einsum('bcpk,cpn->bnk', pooled, rec_weight, precision=highest) + rec_bias[None, :, None]
    new_maps = jnp.tanh(recombined)
    features = jnp.concatenate([fields, new_maps], axis=1)
    gram_grad = gram_block.astype(jnp.float32)
    symmetric = gram_grad + jnp.swapaxes(gram_grad, 1, 2)
    feat_grad = cot_block.astype(jnp.float32) + jnp.einsum('bij,bjk->bik', symmetric, features, precision=highest)
    recomb_grad = feat_grad[:, F:, :] * (1.0 - new_maps * new_maps)
    rec_weight_term = jnp.einsum('bcpk,bnk->cpn', pooled, recomb_grad, precision=highest)
    rec_bias_term = lax.optimization_barrier(jnp.sum(recomb_grad, axis=(0, 2)))
    pooled_grad = jnp.einsum('cpn,bnk->bcpk', rec_weight, recomb_grad, precision=highest)
    tanh_grad = jnp.repeat(0.5 * pooled_grad, 2, axis=2)
    tanh_grad = jnp.pad(tanh_grad, ((0, 0), (0, 0), (0, F - 2 * P_SIZE), (0, 0)))
    conv_grad = tanh_grad * (1.0 - activated * activated)
    conv_weight_term = jnp.einsum('bcik,bdik->cd', conv_grad, shifted, precision=highest)
    conv_bias_term = lax.optimization_barrier(jnp.sum(conv_grad, axis=(0, 2, 3)))
    grad_padded = jnp.pad(conv_grad, ((0, 0), (0, 0), (margin, margin), (0, 0)))
    field_grad = feat_grad[:, :F, :]
    for shift in range(KH):
        window = grad_padded[:, :, KH - 1 - shift:KH - 1 - shift + F, :]
        field_grad = field_grad + jnp.einsum('c,bcik->bik', conv_weight[:, shift], window, precision=highest)
    return (field_grad.astype(jnp.bfloat16), (conv_weight_term, conv_bias_term, rec_weight_term, rec_bias_term))

def reference(pooled_emb, conv_weight, conv_bias, rec_weight, rec_bias, feat_cot, gram_cot, bag_ids, bag_lengths, field_table):
    blocks = N_WIDE * N_REP

    def one_block(packed):
        return dense_backward(packed[0], packed[1], packed[2], conv_weight, conv_bias, rec_weight, rec_bias)
    stacked = (pooled_emb.reshape(blocks, B_DEV, F, K), feat_cot.reshape(blocks, B_DEV, FT, K), gram_cot.reshape(blocks, B_DEV, FT, FT))
    emb_grad, terms = lax.map(one_block, stacked)
    emb_grad = emb_grad.reshape(SAMPLES, F, K)
    grad_scale = 1.0 / math.sqrt(SAMPLES)
    conv_weight_grad = lax.optimization_barrier(jnp.sum(terms[0], axis=0)) * grad_scale
    conv_bias_grad = lax.optimization_barrier(jnp.sum(terms[1], axis=0)) * grad_scale
    rec_weight_grad = lax.optimization_barrier(jnp.sum(terms[2], axis=0)) * grad_scale
    rec_bias_grad = lax.optimization_barrier(jnp.sum(terms[3], axis=0)) * grad_scale
    live_slot = jnp.arange(BAG, dtype=jnp.int32)[None, None, :] < bag_lengths[:, :, None]
    row_index = field_table[None, :, None] * TROWS + bag_ids
    row_index = jnp.where(live_slot, row_index, NT * TROWS).astype(jnp.int32)
    values = jnp.broadcast_to(emb_grad[:, :, None, :], (SAMPLES, F, BAG, K)).reshape(-1, K).astype(jnp.float32)
    summed = jax.ops.segment_sum(values, row_index.reshape(-1), num_segments=NT * TROWS + 1)[:NT * TROWS]
    table_grad = summed.reshape(NT, TROWS, K).transpose(0, 2, 1)
    return (table_grad, conv_weight_grad, conv_bias_grad, rec_weight_grad, rec_bias_grad)
```

```python
import math

import jax
import jax.numpy as jnp
from jax import lax
from jax.experimental import pallas as pl
from jax.experimental.pallas import tpu as pltpu
from jax.sharding import PartitionSpec as P

K = 64
F = 39
NT = 26
C = 14
KH = 7
BAG = 4
B_DEV = 8
T_SHARE = 128
P_SIZE = 19
NF = 57
FT = 96
SAMPLES = 2048
TROWS = 32768
N_WIDE = 64
N_REP = 4

ROWS = C * P_SIZE
RPAD = 272
LANES = B_DEV * K
FPAD = 40
BAGS = B_DEV * FPAD
MSG = 32
SLOT_ROWS = 1280
META = 144
MESH = pl.DeviceIdType.MESH
VMEM_LIMIT = 56 * 1024 * 1024
f32 = jnp.float32
bf16 = jnp.bfloat16
i32 = jnp.int32


def split(x):
    hi = x.astype(bf16)
    return hi, (x - hi.astype(f32)).astype(bf16)


def mm(a, b, contract=((1,), (0,))):
    return lax.dot_general(a, b, (contract, ((), ())), preferred_element_type=f32)


def mm3(a, b, contract=((1,), (0,))):
    return mm(a[0], b[0], contract) + (mm(a[1], b[0], contract) + mm(a[0], b[1], contract))


NT_DIMS = ((1,), (1,))
TN_DIMS = ((0,), (0,))


def iota(shape, dim):
    return lax.broadcasted_iota(i32, shape, dim)


def dense_kernel(cw, cb, emb, cot, gram, rw, rb, ids, send, aux, xs, tz, rws, fs, fg):
    me_x = lax.axis_index("rep")
    me_w = lax.axis_index("wide")
    for m in range(B_DEV // 2):
        pair = jnp.concatenate([emb[2 * m].astype(f32), emb[2 * m + 1].astype(f32)], axis=1)
        xs[0:F, 128 * m : 128 * m + 128] = pair
    xs[F : F + 1, :] = jnp.ones((1, LANES), f32)
    xb = xs[...].astype(bf16)
    p_at = iota((P_SIZE, FPAD), 0)
    j_at = iota((P_SIZE, FPAD), 1)
    bands = [((j_at == 2 * p_at + (m - 3)) & (j_at < F)).astype(f32) for m in range(KH + 1)]
    last = (j_at == F).astype(f32)
    tz[ROWS:RPAD, :] = jnp.zeros((RPAD - ROWS, FPAD), f32)
    tz[RPAD + ROWS :, :] = jnp.zeros((RPAD - ROWS, FPAD), f32)
    rws[...] = jnp.zeros((RPAD, K), f32)
    for c in range(C):
        even = cb[c] * last
        odd = even
        for d in range(KH):
            even = even + cw[c, d] * bands[d]
            odd = odd + cw[c, d] * bands[d + 1]
        tz[c * P_SIZE : (c + 1) * P_SIZE, :] = even
        tz[RPAD + c * P_SIZE : RPAD + (c + 1) * P_SIZE, :] = odd
        rws[c * P_SIZE : (c + 1) * P_SIZE, 0:NF] = rw[c]
    band = tz[...]
    band_s = split(band)
    act = jnp.tanh(mm(band_s[0], xb) + mm(band_s[1], xb))
    act_e = act[:RPAD]
    act_o = act[RPAD:]
    pooled = 0.5 * (act_e + act_o)
    row_at = iota((RPAD, LANES), 0)
    pooled = jnp.where(row_at == ROWS, 1.0, pooled)
    pooled_s = split(pooled)
    rw_only = rws[...]
    rws[ROWS : ROWS + 1, 0:NF] = rb[...]
    rwt_s = split(rws[...].T)
    new_maps = jnp.tanh(mm3(rwt_s, pooled_s))
    fs[0:F, :] = xs[0:F, :]
    fs[F:FT, :] = new_maps[0:NF]
    low = iota((FT, 128), 1) < K
    for m in range(B_DEV // 2):
        pair = fs[:, 128 * m : 128 * m + 128]
        pair_s = jnp.concatenate(split(pair), axis=1)
        halves = []
        for s in (2 * m, 2 * m + 1):
            g = gram[s]
            part = mm(g, pair_s) + mm(g, pair_s, TN_DIMS)
            halves.append(part[:, 0:128] + part[:, 128:256])
        direct = jnp.concatenate([cot[2 * m].astype(f32), cot[2 * m + 1].astype(f32)], axis=1)
        fg[0:FT, 128 * m : 128 * m + 128] = direct + jnp.where(low, halves[0], halves[1])
    fg[FT:, :] = jnp.zeros((8, LANES), f32)
    recg = fg[F : F + K, :] * (1.0 - new_maps * new_maps)
    recg = jnp.where(iota((K, LANES), 0) < NF, recg, 0.0)
    recg_s = split(recg)
    pooled_grad = mm3(split(rw_only), recg_s)
    half = 0.5 * pooled_grad
    conv_grad = jnp.concatenate(
        [half * (1.0 - act_e * act_e), half * (1.0 - act_o * act_o)], axis=0
    )
    cg_s = split(conv_grad)
    emb_grad = fg[0:FPAD, :] + mm3(split(band.T), cg_s)

    low = iota((FPAD, 128), 1) < K
    lows, highs = [], []
    for m in range(B_DEV // 2):
        pair = emb_grad[:, 128 * m : 128 * m + 128]
        other = pltpu.roll(pair, K, 1)
        lows += [jnp.where(low, pair, 0.0), jnp.where(low, other, 0.0)]
        highs += [jnp.where(low, 0.0, other), jnp.where(low, 0.0, pair)]
    bag_rows = jnp.concatenate(lows + highs, axis=0).astype(bf16)

    owner_at = iota((N_WIDE, BAGS), 0)
    values, owners, owned = [], [], []
    count = jnp.zeros((N_WIDE, BAGS), f32)
    for j in range(BAG):
        v = ids[j : j + 1, :]
        w = jnp.where(v >= 0, (v >> 9) & (N_WIDE - 1), -1)
        hit = (owner_at == w).astype(f32)
        values.append(v)
        owners.append(w)
        owned.append(hit)
        count = count + hit
    before = (iota((BAGS, BAGS), 0) < iota((BAGS, BAGS), 1)).astype(f32).astype(bf16)
    ahead = mm(count.astype(bf16), before)
    places = ([], [])
    codes = jnp.zeros((2 * N_WIDE, 128), f32)
    slot_at = iota((128, BAGS), 0)
    tile_at = (me_w & 3) * 4
    for j in range(BAG):
        rank = jnp.sum(owned[j] * ahead, axis=0, keepdims=True).astype(i32)
        ahead = ahead + owned[j]
        v, w = values[j], owners[j]
        late = rank - 32
        row = jnp.where(rank < 32, rank & 15, 16 + tile_at + (late & 3))
        side = jnp.where(rank < 32, rank >> 4, late >> 2)
        at = w * MSG + row
        for h in range(2):
            places[h].append(jnp.where((w >= 0) & (side == h), at, -1))
        first = ((v >> 15) * 4 + ((v >> 7) & 3) + 1).astype(f32)
        second = (v & (T_SHARE - 1)).astype(f32)
        lhs = jnp.concatenate([owned[j] * first, owned[j] * second], axis=0).astype(bf16)
        codes = codes + mm(lhs, (slot_at == rank).astype(f32).astype(bf16), NT_DIMS)
    aux[:, 0, :] = codes[0:N_WIDE] * 128.0 + codes[N_WIDE:]
    group = 8
    for c in range(N_WIDE // group):
        rows_at = iota((group * MSG, BAGS), 0) + c * group * MSG
        picks = []
        for h in range(2):
            hit = rows_at == places[h][0]
            for j in range(1, BAG):
                hit = hit | (rows_at == places[h][j])
            picks.append(hit.astype(f32).astype(bf16))
        rows = mm(jnp.concatenate(picks, axis=1), bag_rows)
        send[c * group : (c + 1) * group] = rows.astype(bf16).reshape(group, MSG, 128)

    rec_term = mm3(pooled_s, recg_s, NT_DIMS)
    cross = mm(cg_s[0], xb, NT_DIMS) + mm(cg_s[1], xb, NT_DIMS)
    row_at = iota((RPAD, FPAD), 0)
    chan = (row_at * 3450) >> 16
    shift = iota((RPAD, FPAD), 1) - 2 * (row_at - chan * P_SIZE) + 3
    inside = iota((RPAD, FPAD), 1) < F
    cross_e, cross_o = cross[:RPAD], cross[RPAD:]
    lane_at = iota((RPAD, 128), 1)
    taps = jnp.where(lane_at == KH, cross_e[:, F : F + 1] + cross_o[:, F : F + 1], 0.0)
    for d in range(KH):
        diag = jnp.where(inside & (shift == d), cross_e, 0.0) + jnp.where(
            inside & (shift == d + 1), cross_o, 0.0
        )
        taps = jnp.where(lane_at == d, jnp.sum(diag, axis=1, keepdims=True), taps)
    chan_at = (iota((16, RPAD), 1) * 3450) >> 16
    pick = (chan_at == iota((16, RPAD), 0)).astype(f32).astype(bf16)
    taps_s = split(taps)
    conv_term = mm(pick, taps_s[0]) + mm(pick, taps_s[1])
    pay = jnp.concatenate([rec_term[0:136], rec_term[136:272]], axis=1)
    aux[:, 1, :] = pay[0:64]
    aux[:, 2, :] = pay[64:128]
    aux[:, 3, :] = jnp.concatenate(
        [pay[128:136], conv_term, jnp.zeros((N_WIDE - 24, 128), f32)], axis=0
    )


def dense(cw, cb, emb, cot, gram, rw, rb, ids):
    smem = pl.BlockSpec(memory_space=pltpu.SMEM)
    vmem = pl.BlockSpec(memory_space=pltpu.VMEM)
    return pl.pallas_call(
        dense_kernel,
        out_shape=(
            jax.ShapeDtypeStruct((N_WIDE, MSG, 128), bf16),
            jax.ShapeDtypeStruct((N_WIDE, 4, 128), f32),
        ),
        in_specs=[smem, smem, vmem, vmem, vmem, vmem, vmem, vmem],
        out_specs=(vmem, vmem),
        scratch_shapes=[
            pltpu.VMEM((FPAD, LANES), f32),
            pltpu.VMEM((2 * RPAD, FPAD), f32),
            pltpu.VMEM((RPAD, K), f32),
            pltpu.VMEM((FT, LANES), f32),
            pltpu.VMEM((FT + 8, LANES), f32),
        ],
        compiler_params=pltpu.CompilerParams(vmem_limit_bytes=VMEM_LIMIT),
        name="dense_pack",
    )(cw, cb, emb, cot, gram, rw, rb, ids)


def exchange_kernel(send, aux, vt, red, rdat, raux, part, parts, sems):
    me_w = lax.axis_index("wide")
    me_x = lax.axis_index("rep")

    def peer(o):
        return lax.rem(me_w + o, N_WIDE)

    def wide_copy(src, dst, to, s, r):
        return pltpu.make_async_remote_copy(
            src_ref=src, dst_ref=dst, send_sem=sems.at[s], recv_sem=sems.at[r],
            device_id=(to, me_x), device_id_type=MESH,
        )

    def rep_copy(src, dst, o, s, r):
        return pltpu.make_async_remote_copy(
            src_ref=src, dst_ref=dst, send_sem=sems.at[s], recv_sem=sems.at[r],
            device_id=(me_w, lax.rem(me_x + o, N_REP)), device_id_type=MESH,
        )

    def wait_bytes(ref, n, s):
        pltpu.make_async_copy(ref.at[pl.ds(0, n)], ref.at[pl.ds(0, n)], sems.at[s]).wait()

    barrier = pltpu.get_barrier_semaphore()

    def greet(o, carry):
        pl.semaphore_signal(barrier, inc=1, device_id=(peer(o), me_x), device_id_type=MESH)
        return carry

    lax.fori_loop(1, N_WIDE, greet, 0)
    for o in range(1, N_REP):
        pl.semaphore_signal(
            barrier, inc=1, device_id=(me_w, lax.rem(me_x + o, N_REP)), device_id_type=MESH
        )
    pl.semaphore_wait(barrier, N_WIDE - 1 + N_REP - 1)

    def start_all(o, carry):
        to = peer(o)
        wide_copy(aux.at[to], raux.at[me_w], to, 0, 1).start()
        wide_copy(send.at[to], rdat.at[me_w], to, 2, 3).start()
        return carry

    lax.fori_loop(1, N_WIDE, start_all, 0)
    raux[me_w] = aux[me_w]
    rdat[me_w] = send[me_w]

    wait_bytes(raux, N_WIDE - 1, 1)
    part[...] = jnp.sum(raux[...], axis=0)
    for o in range(1, N_REP):
        rep_copy(part, parts.at[me_x], o, 4, 5).start()
    parts[me_x] = part[...]

    codes = raux[:, 0, :]
    lane = iota((N_WIDE, 128), 1)
    src = iota((N_WIDE, 128), 0)
    flat = []
    for h in range(2):
        near = pltpu.roll(codes, 128 - 16 * h, 1) if h else codes
        near = jnp.where(lane < 16, near, 0.0)
        for by in (16, 32, 64):
            near = near + pltpu.roll(near, by, 1)
        near = jnp.where((lane >> 4) == (src & 7), near, 0.0)
        near = jnp.sum(near.reshape(8, 8, 128), axis=1)
        late = pltpu.roll(codes, 128 - 32 - 4 * h, 1)
        late = jnp.where(lane < 4, late, 0.0)
        for by in (4, 8, 16, 32, 64):
            late = late + pltpu.roll(late, by, 1)
        late = jnp.where((lane >> 2) == (src & 31), late, 0.0)
        late = jnp.sum(late.reshape(2, 32, 128), axis=1)
        flat.append(jnp.concatenate([near, late], axis=0))
    high = [jnp.floor(x * (1.0 / 128.0)) for x in flat]
    small = [x - 128.0 * y for x, y in zip(flat, high)]
    meta_at = iota((16, 128), 0)
    for g in range(10):
        rows = jnp.zeros((16, 128), f32)
        for n, x in enumerate((high[0], small[0], high[1], small[1])):
            rows = jnp.where(meta_at == n, x[g : g + 1, :], rows)
        vt[me_x, 128:META, 128 * g : 128 * g + 128] = rows.astype(bf16)

    wait_bytes(rdat, N_WIDE - 1, 3)
    for g in range(8):
        rows = rdat[8 * g : 8 * g + 8, 0:16, :].reshape(128, 128).astype(f32)
        vt[me_x, 0:128, 128 * g : 128 * g + 128] = rows.T.astype(bf16)
    for e in range(2):
        rows = rdat[32 * e : 32 * e + 32, 16:32, :].astype(f32)
        rows = jnp.sum(rows.reshape(8, 4, 16, 128), axis=1).reshape(128, 128)
        vt[me_x, 0:128, 1024 + 128 * e : 1024 + 128 * e + 128] = rows.T.astype(bf16)
    for o in range(1, N_REP):
        rep_copy(vt.at[me_x], vt.at[me_x], o, 6, 7).start()

    wait_bytes(parts, N_REP - 1, 5)
    red[me_w] = (parts[0] + parts[1]) + (parts[2] + parts[3])

    def start_sums(o, carry):
        wide_copy(red.at[me_w], red.at[me_w], peer(o), 8, 9).start()
        return carry

    lax.fori_loop(1, N_WIDE, start_sums, 0)
    wait_bytes(red, N_WIDE - 1, 9)
    wait_bytes(red, N_WIDE - 1, 8)
    wait_bytes(raux, N_WIDE - 1, 0)
    wait_bytes(rdat, N_WIDE - 1, 2)
    wait_bytes(parts, N_REP - 1, 4)
    wait_bytes(vt, N_REP - 1, 7)
    wait_bytes(vt, N_REP - 1, 6)


def exchange(send, aux):
    vmem = pl.BlockSpec(memory_space=pltpu.VMEM)
    return pl.pallas_call(
        exchange_kernel,
        out_shape=(
            jax.ShapeDtypeStruct((N_REP, META, SLOT_ROWS), bf16),
            jax.ShapeDtypeStruct((N_WIDE, 4, 128), f32),
        ),
        in_specs=[vmem, vmem],
        out_specs=(vmem, vmem),
        scratch_shapes=[
            pltpu.VMEM((N_WIDE, MSG, 128), bf16),
            pltpu.VMEM((N_WIDE, 4, 128), f32),
            pltpu.VMEM((4, 128), f32),
            pltpu.VMEM((N_REP, 4, 128), f32),
            pltpu.SemaphoreType.DMA((10,)),
        ],
        compiler_params=pltpu.CompilerParams(
            vmem_limit_bytes=VMEM_LIMIT, collective_id=0, has_side_effects=True
        ),
        name="exchange",
    )(send, aux)


def gather_kernel(scale, vt, red, table, conv_w, conv_b, rec_w, rec_b, acc, pays, wide_w):
    me_x = lax.axis_index("rep")
    row_at = iota((256, SLOT_ROWS), 0)
    for x in range(N_REP):
        for h in range(2):
            rows = vt[x, K * h : K * h + K, :]
            meta = vt[x, 128:META, :].astype(f32).astype(i32)
            code = meta[2 * h : 2 * h + 1, :] - 1
            table_at = code >> 2
            mine = (code >= 0) & ((code & 3) == me_x)
            target = jnp.where(
                mine, (table_at & 1) * T_SHARE + meta[2 * h + 1 : 2 * h + 2, :], -1
            )
            hits = (row_at == target).astype(f32).astype(bf16)
            pair_at = table_at >> 1
            spread = jnp.concatenate(
                [rows * (pair_at == t).astype(f32).astype(bf16) for t in range(NT // 2)], axis=0
            )
            term = mm(spread, hits, NT_DIMS)
            if x == 0 and h == 0:
                acc[...] = term
            else:
                acc[...] += term
    for t in range(NT):
        half = (t % 2) * T_SHARE
        table[t] = acc[(t // 2) * K : (t // 2) * K + K, half : half + T_SHARE]

    for g in range(3):
        pays[64 * g : 64 * g + 64, :] = red[:, 1 + g, :] * scale
    wide_w[0:136, :] = pays[0:136, :]
    wide_w[136:272, :] = pltpu.roll(pays[0:136, :], K, 1)
    for c in range(C):
        rec_w[c] = wide_w[c * P_SIZE : (c + 1) * P_SIZE, 0:NF]
    rec_b[...] = wide_w[ROWS : ROWS + 1, 0:NF]
    conv = pays[136:152, :]
    conv_w[...] = conv[0:C, 0:KH]
    square = iota((16, 128), 0) == iota((16, 128), 1)
    bias = jnp.sum(jnp.where(square, conv[:, KH : KH + 1], 0.0), axis=0, keepdims=True)
    conv_b[...] = bias[:, 0:C]


def gather(scale, vt, red):
    vmem = pl.BlockSpec(memory_space=pltpu.VMEM)

    def kernel(*refs):
        gather_kernel(scale, *refs)

    return pl.pallas_call(
        kernel,
        out_shape=(
            jax.ShapeDtypeStruct((NT, K, T_SHARE), f32),
            jax.ShapeDtypeStruct((C, KH), f32),
            jax.ShapeDtypeStruct((1, C), f32),
            jax.ShapeDtypeStruct((C, P_SIZE, NF), f32),
            jax.ShapeDtypeStruct((1, NF), f32),
        ),
        in_specs=[vmem, vmem],
        out_specs=(vmem,) * 5,
        scratch_shapes=[
            pltpu.VMEM((NT // 2 * K, 256), f32),
            pltpu.VMEM((192, 128), f32),
            pltpu.VMEM((RPAD, 128), f32),
        ],
        compiler_params=pltpu.CompilerParams(vmem_limit_bytes=VMEM_LIMIT),
        name="table_rows",
    )(vt, red)


def slot_values(bag_ids, bag_lengths, field_table):
    live = jnp.arange(BAG, dtype=i32)[None, None, :] < bag_lengths[:, :, None]
    value = jnp.where(live, field_table[None, :, None] * TROWS + bag_ids, -1)
    value = jnp.pad(value, ((0, 0), (0, FPAD - F), (0, 0)), constant_values=-1)
    return value.transpose(2, 0, 1).reshape(BAG, BAGS)


def local(
    pooled_emb, conv_weight, conv_bias, rec_weight, rec_bias, feat_cot, gram_cot, bag_ids,
    bag_lengths, field_table,
):
    ids = slot_values(bag_ids, bag_lengths, field_table)
    send, aux = dense(
        conv_weight, conv_bias, pooled_emb, feat_cot, gram_cot, rec_weight,
        rec_bias.reshape(1, NF), ids,
    )
    vt, red = exchange(send, aux)
    table, conv_w, conv_b, rec_w, rec_b = gather(1.0 / math.sqrt(SAMPLES), vt, red)
    return table, conv_w, conv_b.reshape(C), rec_w, rec_b.reshape(NF)


def solution(mesh):
    in_specs = (
        P(("wide", "rep"), None, None), P(), P(), P(), P(), P(("wide", "rep"), None, None),
        P(("wide", "rep"), None, None), P(("wide", "rep"), None, None), P(("wide", "rep"), None),
        P(),
    )
    out_specs = (P(None, None, ("wide", "rep")), P(), P(), P(), P())
    return jax.shard_map(local, mesh=mesh, in_specs=in_specs, out_specs=out_specs, check_vma=False)
```

```python
import math

import jax
import jax.numpy as jnp
from jax import lax
from jax.experimental import pallas as pl
from jax.experimental.pallas import tpu as pltpu
from jax.sharding import PartitionSpec as P

K = 64
F = 39
NT = 26
C = 14
KH = 7
BAG = 4
B_DEV = 8
T_SHARE = 128
P_SIZE = 19
NF = 57
FT = 96
SAMPLES = 2048
TROWS = 32768
N_WIDE = 64
N_REP = 4

ROWS = C * P_SIZE
RPAD = 272
LANES = B_DEV * K
FPAD = 40
BAGS = B_DEV * FPAD
MSG = 24
GROUPS = 4
CHUNKS = GROUPS + 1
BLOCK = 72
MESH = pl.DeviceIdType.MESH
VMEM_LIMIT = 56 * 1024 * 1024
f32 = jnp.float32
bf16 = jnp.bfloat16
i32 = jnp.int32


def split(x):
    hi = x.astype(bf16)
    return hi, (x - hi.astype(f32)).astype(bf16)


def mm(a, b, contract=((1,), (0,))):
    return lax.dot_general(a, b, (contract, ((), ())), preferred_element_type=f32)


def mm3(a, b, contract=((1,), (0,))):
    return mm(a[0], b[0], contract) + (mm(a[1], b[0], contract) + mm(a[0], b[1], contract))


NT_DIMS = ((1,), (1,))
TN_DIMS = ((0,), (0,))


def iota(shape, dim):
    return lax.broadcasted_iota(i32, shape, dim)


def dense_part(
    me_w, cw, cb, emb, cot, gram, rw, rb, ids, lengths, field_table,
    send, stage, es, xs, tz, rws, fs, fg, ip,
):
    es[:, 0:K] = emb[...].astype(f32).reshape(F * B_DEV, K)
    for m in range(B_DEV // 2):
        pair = [es[pl.ds(2 * m + e, F, stride=B_DEV), :][:, 0:K] for e in range(2)]
        xs[0:F, 128 * m : 128 * m + 128] = jnp.concatenate(pair, axis=1)
    xs[F : F + 1, :] = jnp.ones((1, LANES), f32)
    xb = xs[...].astype(bf16)
    taps = jnp.concatenate([cw[...], cb[...]], axis=0).T
    taps = jnp.concatenate([taps, jnp.zeros((C, 120), f32)], axis=1)
    lane = iota((C, 128), 1)
    kernel_taps = jnp.where(lane < KH, taps, 0.0)
    bias_tap = pltpu.roll(jnp.where(lane == KH, taps, 0.0), F - KH, 1)
    tz[ROWS:RPAD, :] = jnp.zeros((RPAD - ROWS, 128), f32)
    tz[RPAD + ROWS :, :] = jnp.zeros((RPAD - ROWS, 128), f32)
    rws[...] = jnp.zeros((RPAD, K), f32)
    for p in range(P_SIZE):
        for odd in range(2):
            moved = pltpu.roll(kernel_taps, (2 * p + odd - 3) % 128, 1)
            rows = pl.ds(odd * RPAD + p * C, C)
            tz[rows, :] = jnp.where(lane < F, moved, 0.0) + bias_tap
        rws[p * C : (p + 1) * C, 0:NF] = rw[p]
    band = tz[:, 0:FPAD]
    band_s = split(band)
    act = jnp.tanh(mm(band_s[0], xb) + mm(band_s[1], xb))
    act_e = act[:RPAD]
    act_o = act[RPAD:]
    pooled = 0.5 * (act_e + act_o)
    pooled = jnp.where(iota((RPAD, LANES), 0) == ROWS, 1.0, pooled)
    pooled_s = split(pooled)
    rw_only = rws[...]
    rws[ROWS : ROWS + 1, 0:NF] = rb[...]
    rwt_s = split(rws[...].T)
    new_maps = jnp.tanh(mm3(rwt_s, pooled_s))
    fs[0:F, :] = xs[0:F, :]
    fs[F:FT, :] = new_maps[0:NF]
    fg[0:FT, :] = cot[...].astype(f32).reshape(LANES, FT).T
    low = iota((FT, 128), 1) < K
    for m in range(B_DEV // 2):
        pair_s = jnp.concatenate(split(fs[:, 128 * m : 128 * m + 128]), axis=1)
        halves = []
        for s in (2 * m, 2 * m + 1):
            g = gram[s]
            part = mm(g, pair_s) + mm(g, pair_s, TN_DIMS)
            halves.append(part[:, 0:128] + part[:, 128:256])
        fg[0:FT, 128 * m : 128 * m + 128] += jnp.where(low, halves[0], halves[1])
    fg[FT:, :] = jnp.zeros((8, LANES), f32)
    recg = fg[F : F + K, :] * (1.0 - new_maps * new_maps)
    recg = jnp.where(iota((K, LANES), 0) < NF, recg, 0.0)
    recg_s = split(recg)
    half = 0.5 * mm3(split(rw_only), recg_s)
    conv_grad = jnp.concatenate(
        [half * (1.0 - act_e * act_e), half * (1.0 - act_o * act_o)], axis=0
    )
    cg_s = split(conv_grad)
    emb_grad = fg[0:FPAD, :] + mm3(split(band.T), cg_s)

    low = iota((FPAD, 128), 1) < K
    lows, highs = [], []
    for m in range(B_DEV // 2):
        pair = emb_grad[:, 128 * m : 128 * m + 128]
        other = pltpu.roll(pair, K, 1)
        lows += [jnp.where(low, pair, 0.0), jnp.where(low, other, 0.0)]
        highs += [jnp.where(low, 0.0, other), jnp.where(low, 0.0, pair)]
    bag_rows = jnp.concatenate(lows + highs, axis=0).astype(bf16)

    ip[...] = jnp.zeros((B_DEV, 8, 128), i32)
    slot_at = iota((BAG, F), 0)
    for s in range(B_DEV):
        live = slot_at < lengths[s : s + 1, :]
        ip[s, 0:BAG, 0:F] = jnp.where(live, field_table[...] * TROWS + ids[s] + 1, 0)
    value = jnp.zeros((8, 384), i32)
    for s in range(B_DEV):
        wide = jnp.concatenate([ip[s], jnp.zeros((8, 256), i32)], axis=1)
        value = value + (pltpu.roll(wide, FPAD * s, 1) if s else wide)
    value = value[:, 0:BAGS] - 1

    peer_at = iota((N_WIDE, BAGS), 0)
    values, offsets, owned = [], [], []
    count = jnp.zeros((N_WIDE, BAGS), f32)
    for j in range(BAG):
        v = value[j : j + 1, :]
        o = jnp.where(v >= 0, ((v >> 9) - me_w) & (N_WIDE - 1), -1)
        hit = (peer_at == o).astype(f32)
        values.append(v)
        offsets.append(o)
        owned.append(hit)
        count = count + hit
    before = (iota((BAGS, BAGS), 0) < iota((BAGS, BAGS), 1)).astype(f32).astype(bf16)
    ahead = mm(count.astype(bf16), before)
    near, late = [], []
    codes = jnp.zeros((2 * N_WIDE, 128), f32)
    slot_at = iota((128, BAGS), 0)
    for j in range(BAG):
        rank = jnp.sum(owned[j] * ahead, axis=0, keepdims=True).astype(i32)
        ahead = ahead + owned[j]
        v, o = values[j], offsets[j]
        early = (o >= 0) & (rank < 32)
        after = (o >= 0) & (rank >= 32)
        rest = rank - 32
        near.append(jnp.concatenate(
            [jnp.where(early & ((rank >> 4) == h), o * 16 + (rank & 15), -1) for h in range(2)], axis=1
        ))
        late.append(jnp.concatenate(
            [jnp.where(after & ((rest >> 2) == h), o * 4 + (rest & 3), -1) for h in range(2)], axis=1
        ))
        first = ((v >> 15) * 4 + ((v >> 7) & 3) + 1).astype(f32)
        second = (v & (T_SHARE - 1)).astype(f32)
        lhs = jnp.concatenate([owned[j] * first, owned[j] * second], axis=0).astype(bf16)
        codes = codes + mm(lhs, (slot_at == rank).astype(f32).astype(bf16), NT_DIMS)

    def pick(rows_at, places):
        hit = rows_at == places[0]
        for j in range(1, BAG):
            hit = hit | (rows_at == places[j])
        return mm(hit.astype(f32).astype(bf16), bag_rows)

    stage[...] = jnp.zeros((N_WIDE, 8, 128), f32)
    stage[:, 0:4, :] = pick(iota((256, 2 * BAGS), 0), late).reshape(N_WIDE, 4, 128)
    stage[:, 4, :] = codes[0:N_WIDE] + pltpu.roll(codes[N_WIDE:], K, 1)
    send[:, 16:24, :] = stage[...].astype(bf16)
    for c in range(GROUPS):
        rows = pick(iota((256, 2 * BAGS), 0) + 256 * c, near)
        send[16 * c : 16 * c + 16, 0:16, :] = rows.astype(bf16).reshape(16, 16, 128)
    return xb, pooled_s, recg_s, cg_s


def weight_part(xb, pooled_s, recg_s, cg_s, aux, tz):
    rec_term = mm3(pooled_s, recg_s, NT_DIMS)
    cross = mm(cg_s[0], xb, NT_DIMS) + mm(cg_s[1], xb, NT_DIMS)
    tz[:, 0:FPAD] = cross
    lane = iota((C, 128), 1)
    taps = jnp.zeros((C, 128), f32)
    bias = jnp.zeros((C, 128), f32)
    for p in range(P_SIZE):
        for odd in range(2):
            rows = tz[pl.ds(odd * RPAD + p * C, C), :]
            bias = bias + rows
            taps = taps + pltpu.roll(jnp.where(lane < F, rows, 0.0), (3 - 2 * p - odd) % 128, 1)
    bias = pltpu.roll(jnp.where(lane == F, bias, 0.0), 128 - F + KH, 1)
    taps = jnp.where(lane < KH, taps, 0.0) + bias
    taps = jnp.concatenate([taps, jnp.zeros((128 - C, 128), f32)], axis=0).T[0:8]
    pay = jnp.concatenate([rec_term[0:136], rec_term[136:272]], axis=1)
    aux[:, 0, :] = pay[0:64]
    aux[:, 1, :] = pay[64:128]
    aux[:, 2, :] = jnp.concatenate(
        [pay[128:136], taps, jnp.zeros((N_WIDE - 16, 128), f32)], axis=0
    )


def windows(codes, first, width):
    n = codes.shape[0]
    lane = iota((n, 128), 1)
    src = iota((n, 128), 0)
    out = pltpu.roll(codes, (128 - first) % 128, 1) if first % 128 else codes
    out = jnp.where(lane < width, out, 0.0)
    by = width
    while by < 128:
        out = out + pltpu.roll(out, by, 1)
        by *= 2
    per = 128 // width
    out = jnp.where(lane // width == (src & (per - 1)), out, 0.0)
    out = jnp.sum(out.reshape(n // per, per, 128), axis=1)
    return jnp.concatenate([out[g : g + 1] for g in range(n // per)], axis=1)


def fill_chunk(vt, g, rows, codes, starts, width):
    turned = rows.T
    row_at = iota((8, 256), 0)
    for h in range(2):
        first = windows(codes, starts[h], width)
        second = windows(codes, 64 + starts[h], width)
        meta = jnp.where(row_at == 0, first, jnp.where(row_at == 1, second, 0.0))
        vt[0, g, h] = jnp.concatenate([turned[K * h : K * h + K], meta], axis=0).astype(bf16)


def add_rows(me_x, vt, acc, slot, g):
    meta = [vt[slot, g, h][K:BLOCK].astype(f32) for h in range(2)]
    rows = jnp.concatenate([vt[slot, g, h][0:K] for h in range(2)], axis=1)
    code = jnp.concatenate([m[0:1] for m in meta], axis=1).astype(i32) - 1
    place = jnp.concatenate([m[1:2] for m in meta], axis=1).astype(i32)
    table_at = code >> 2
    mine = (code >= 0) & ((code & 3) == me_x)
    target = jnp.where(mine, (table_at & 1) * T_SHARE + place, -1)
    hits = (iota((256, 512), 0) == target).astype(f32).astype(bf16)
    pair_at = table_at >> 1
    spread = jnp.concatenate(
        [rows * (pair_at == t).astype(f32).astype(bf16) for t in range(NT // 2)], axis=0
    )
    acc[...] += mm(spread, hits, NT_DIMS)


def whole_kernel(
    cw, cb, emb, cot, gram, rw, rb, ids, lengths, field_table,
    table, conv_w, conv_b, rec_w, rec_b,
    send, stage, es, xs, tz, rws, fs, fg, ip, aux,
    rdat, raux, part, parts, red, vt, acc, pays, wide_w,
    data_sems, ring_recv, ring_send, sems,
):
    me_w = lax.axis_index("wide")
    me_x = lax.axis_index("rep")
    right = lax.rem(me_x + 1, N_REP)
    left = lax.rem(me_x + N_REP - 1, N_REP)

    def peer(o):
        return lax.rem(me_w + o, N_WIDE)

    def wide_copy(src, dst, to, s, r):
        return pltpu.make_async_remote_copy(
            src_ref=src, dst_ref=dst, send_sem=s, recv_sem=r,
            device_id=(to, me_x), device_id_type=MESH,
        )

    def rep_copy(src, dst, to, s, r):
        return pltpu.make_async_remote_copy(
            src_ref=src, dst_ref=dst, send_sem=s, recv_sem=r,
            device_id=(me_w, to), device_id_type=MESH,
        )

    def wait_bytes(ref, n, sem):
        pltpu.make_async_copy(ref.at[pl.ds(0, n)], ref.at[pl.ds(0, n)], sem).wait()

    barrier = pltpu.get_barrier_semaphore()

    def greet(o, carry):
        pl.semaphore_signal(barrier, inc=1, device_id=(peer(o), me_x), device_id_type=MESH)
        return carry

    lax.fori_loop(1, N_WIDE, greet, 0)
    for o in range(1, N_REP):
        pl.semaphore_signal(
            barrier, inc=1, device_id=(me_w, lax.rem(me_x + o, N_REP)), device_id_type=MESH
        )

    terms = dense_part(
        me_w, cw, cb, emb, cot, gram, rw, rb, ids, lengths, field_table,
        send, stage, es, xs, tz, rws, fs, fg, ip,
    )
    pl.semaphore_wait(barrier, N_WIDE - 1 + N_REP - 1)

    def send_rows(o, carry):
        wide_copy(
            send.at[o], rdat.at[o], peer(o), sems.at[0], data_sems.at[o // 16]
        ).start()
        return carry

    def send_terms(o, carry):
        to = peer(o)
        wide_copy(aux.at[to], raux.at[me_w], to, sems.at[1], sems.at[2]).start()
        return carry

    def send_sums(o, carry):
        wide_copy(red.at[me_w], red.at[me_w], peer(o), sems.at[5], sems.at[6]).start()
        return carry

    lax.fori_loop(1, SPLIT_AT, send_rows, 0)
    weight_part(*terms, aux, tz)
    lax.fori_loop(1, N_WIDE, send_terms, 0)
    lax.fori_loop(SPLIT_AT, N_WIDE, send_rows, 0)
    rdat[0] = send[0]
    raux[me_w] = aux[me_w]
    acc[...] = jnp.zeros(acc.shape, f32)

    def ring(kind, g):
        slot, h, to, there = (
            (0, 0, right, 1), (0, 1, right, 1), (0, 1, left, 2), (0, 0, left, 2),
            (1, 0, right, 3), (2, 1, left, 3),
        )[kind]
        return rep_copy(
            vt.at[slot, g, h], vt.at[there, g, h], to, ring_send.at[kind], ring_recv.at[kind, g]
        )

    def step(g, carry):
        @pl.when(g < GROUPS)
        def _():
            @pl.when(g == 0)
            def _():
                wait_bytes(rdat, 15, data_sems.at[0])

            @pl.when(g > 0)
            def _():
                wait_bytes(rdat, 16, data_sems.at[g])

            got = rdat[pl.ds(16 * g, 16)]
            rows = got[:, 0:16, :].reshape(256, 128).astype(f32)
            codes = got[:, 16:24, :].astype(f32)[:, 4, :]
            fill_chunk(vt, g, rows, codes, (0, 16), 16)

        @pl.when(g == GROUPS)
        def _():
            tail = rdat[:, 16:24, :].astype(f32)
            rows = tail[:, 0:4, :].reshape(256, 128)
            fill_chunk(vt, GROUPS, rows, tail[:, 4, :], (32, 36), 4)

        @pl.when(g < CHUNKS)
        def _():
            for kind in (0, 2, 1, 3):
                ring(kind, g).start()

        @pl.when((g >= 1) & (g <= CHUNKS))
        def _():
            ring(0, g - 1).wait_recv()
            ring(4, g - 1).start()
            ring(2, g - 1).wait_recv()
            ring(5, g - 1).start()

        @pl.when(g < CHUNKS)
        def _():
            add_rows(me_x, vt, acc, 0, g)

        @pl.when(g == 2)
        def _():
            wait_bytes(raux, N_WIDE - 1, sems.at[2])
            part[...] = jnp.sum(raux[...], axis=0)
            for o in range(1, N_REP):
                to = lax.rem(me_x + o, N_REP)
                rep_copy(part, parts.at[me_x], to, sems.at[3], sems.at[4]).start()
            parts[me_x] = part[...]

        @pl.when((g >= 1) & (g <= CHUNKS))
        def _():
            ring(1, g - 1).wait_recv()
            ring(3, g - 1).wait_recv()
            add_rows(me_x, vt, acc, 1, g - 1)
            add_rows(me_x, vt, acc, 2, g - 1)

        @pl.when(g == 2)
        def _():
            wait_bytes(parts, N_REP - 1, sems.at[4])
            red[me_w] = (parts[0] + parts[1]) + (parts[2] + parts[3])
            lax.fori_loop(1, N_WIDE, send_sums, 0)

        @pl.when(g >= 2)
        def _():
            ring(4, g - 2).wait_recv()
            ring(5, g - 2).wait_recv()
            add_rows(me_x, vt, acc, 3, g - 2)

        return carry

    lax.fori_loop(0, CHUNKS + 2, step, 0)

    for t in range(NT):
        half = (t % 2) * T_SHARE
        table[t] = acc[(t // 2) * K : (t // 2) * K + K, half : half + T_SHARE]

    wait_bytes(red, N_WIDE - 1, sems.at[6])
    scale = 1.0 / math.sqrt(SAMPLES)
    for g in range(3):
        pays[64 * g : 64 * g + 64, :] = red[:, g, :] * scale
    wide_w[0:136, :] = pays[0:136, :]
    wide_w[136:272, :] = pltpu.roll(pays[0:136, :], K, 1)
    for p in range(P_SIZE):
        rec_w[p] = wide_w[p * C : (p + 1) * C, 0:NF]
    rec_b[...] = wide_w[ROWS : ROWS + 1, 0:NF]
    conv_w[...] = pays[136 : 136 + KH, 0:C]
    conv_b[...] = pays[136 + KH : 137 + KH, 0:C]

    wait_bytes(red, N_WIDE - 1, sems.at[5])
    wait_bytes(raux, N_WIDE - 1, sems.at[1])
    wait_bytes(rdat, N_WIDE - 1, sems.at[0])
    wait_bytes(parts, N_REP - 1, sems.at[3])
    for kind in range(6):
        for g in range(CHUNKS):
            ring(kind, g).wait_send()


SPLIT_AT = 32


def local(
    pooled_emb, conv_weight, conv_bias, rec_weight, rec_bias, feat_cot, gram_cot, bag_ids,
    bag_lengths, field_table,
):
    vmem = pl.BlockSpec(memory_space=pltpu.VMEM)
    table, conv_w, conv_b, rec_w, rec_b = pl.pallas_call(
        whole_kernel,
        out_shape=(
            jax.ShapeDtypeStruct((NT, K, T_SHARE), f32),
            jax.ShapeDtypeStruct((KH, C), f32),
            jax.ShapeDtypeStruct((1, C), f32),
            jax.ShapeDtypeStruct((P_SIZE, C, NF), f32),
            jax.ShapeDtypeStruct((1, NF), f32),
        ),
        in_specs=[vmem] * 10,
        out_specs=(vmem,) * 5,
        scratch_shapes=[
            pltpu.VMEM((N_WIDE, MSG, 128), bf16),
            pltpu.VMEM((N_WIDE, 8, 128), f32),
            pltpu.VMEM((F * B_DEV, 128), f32),
            pltpu.VMEM((FPAD, LANES), f32),
            pltpu.VMEM((2 * RPAD, 128), f32),
            pltpu.VMEM((RPAD, K), f32),
            pltpu.VMEM((FT, LANES), f32),
            pltpu.VMEM((FT + 8, LANES), f32),
            pltpu.VMEM((B_DEV, 8, 128), i32),
            pltpu.VMEM((N_WIDE, 3, 128), f32),
            pltpu.VMEM((N_WIDE, MSG, 128), bf16),
            pltpu.VMEM((N_WIDE, 3, 128), f32),
            pltpu.VMEM((3, 128), f32),
            pltpu.VMEM((N_REP, 3, 128), f32),
            pltpu.VMEM((N_WIDE, 3, 128), f32),
            pltpu.VMEM((N_REP, CHUNKS, 2, BLOCK, 256), bf16),
            pltpu.VMEM((NT // 2 * K, 256), f32),
            pltpu.VMEM((192, 128), f32),
            pltpu.VMEM((RPAD, 128), f32),
            pltpu.SemaphoreType.DMA((GROUPS,)),
            pltpu.SemaphoreType.DMA((6, CHUNKS)),
            pltpu.SemaphoreType.DMA((6,)),
            pltpu.SemaphoreType.DMA((7,)),
        ],
        compiler_params=pltpu.CompilerParams(
            vmem_limit_bytes=VMEM_LIMIT, collective_id=0, has_side_effects=True
        ),
        name="whole",
    )(
        conv_weight.T, conv_bias.reshape(1, C), pooled_emb.transpose(1, 0, 2),
        feat_cot.transpose(0, 2, 1), gram_cot, rec_weight.transpose(1, 0, 2),
        rec_bias.reshape(1, NF), bag_ids.transpose(0, 2, 1), bag_lengths,
        field_table.reshape(1, F),
    )
    return table, conv_w.T, conv_b.reshape(C), rec_w.transpose(1, 0, 2), rec_b.reshape(NF)


def solution(mesh):
    in_specs = (
        P(("wide", "rep"), None, None), P(), P(), P(), P(), P(("wide", "rep"), None, None),
        P(("wide", "rep"), None, None), P(("wide", "rep"), None, None), P(("wide", "rep"), None),
        P(),
    )
    out_specs = (P(None, None, ("wide", "rep")), P(), P(), P(), P())
    return jax.shard_map(local, mesh=mesh, in_specs=in_specs, out_specs=out_specs, check_vma=False)
```

```python
import math

import jax
import jax.numpy as jnp
from jax import lax
from jax.experimental import pallas as pl
from jax.experimental.pallas import tpu as pltpu
from jax.sharding import PartitionSpec as P

K = 64
F = 39
NT = 26
C = 14
KH = 7
BAG = 4
B_DEV = 8
T_SHARE = 128
P_SIZE = 19
NF = 57
FT = 96
SAMPLES = 2048
TROWS = 32768
N_WIDE = 64
N_REP = 4

ROWS = C * P_SIZE
RPAD = 272
LANES = B_DEV * K
FPAD = 40
BAGS = B_DEV * FPAD
MSG = 24
PARTNERS = sorted(
    ((y, z, c) for y in range(4) for z in range(8) for c in range(2)),
    key=lambda at: (min(at[0], 4 - at[0]) + min(at[1], 8 - at[1]), at),
)
GROUPS = 4
CHUNKS = GROUPS + 1
BLOCK = 72
MESH = pl.DeviceIdType.MESH
VMEM_LIMIT = 56 * 1024 * 1024
f32 = jnp.float32
bf16 = jnp.bfloat16
i32 = jnp.int32


def split(x):
    hi = x.astype(bf16)
    return hi, (x - hi.astype(f32)).astype(bf16)


def mm(a, b, contract=((1,), (0,))):
    return lax.dot_general(a, b, (contract, ((), ())), preferred_element_type=f32)


def mm3(a, b, contract=((1,), (0,))):
    return mm(a[0], b[0], contract) + (mm(a[1], b[0], contract) + mm(a[0], b[1], contract))


NT_DIMS = ((1,), (1,))
TN_DIMS = ((0,), (0,))


def iota(shape, dim):
    return lax.broadcasted_iota(i32, shape, dim)


def dense_part(
    me, cw, cb, emb, cot, gram, rw, rb, ids, lengths, field_table, order,
    send, stage, es, xs, tz, rws, fs, fg, ip, weight_terms,
):
    es[:, 0:K] = emb[...].astype(f32).reshape(F * B_DEV, K)
    for m in range(B_DEV // 2):
        pair = [es[pl.ds(2 * m + e, F, stride=B_DEV), :][:, 0:K] for e in range(2)]
        xs[0:F, 128 * m : 128 * m + 128] = jnp.concatenate(pair, axis=1)
    xs[F : F + 1, :] = jnp.ones((1, LANES), f32)
    xb = xs[...].astype(bf16)
    taps = jnp.concatenate([cw[...], cb[...]], axis=0).T
    taps = jnp.concatenate([taps, jnp.zeros((C, 120), f32)], axis=1)
    lane = iota((C, 128), 1)
    kernel_taps = jnp.where(lane < KH, taps, 0.0)
    bias_tap = pltpu.roll(jnp.where(lane == KH, taps, 0.0), F - KH, 1)
    tz[ROWS:RPAD, :] = jnp.zeros((RPAD - ROWS, 128), f32)
    tz[RPAD + ROWS :, :] = jnp.zeros((RPAD - ROWS, 128), f32)
    rws[...] = jnp.zeros((RPAD, K), f32)
    for p in range(P_SIZE):
        for odd in range(2):
            moved = pltpu.roll(kernel_taps, (2 * p + odd - 3) % 128, 1)
            rows = pl.ds(odd * RPAD + p * C, C)
            tz[rows, :] = jnp.where(lane < F, moved, 0.0) + bias_tap
        rws[p * C : (p + 1) * C, 0:NF] = rw[p]
    band = tz[:, 0:FPAD]
    band_s = split(band)
    act = jnp.tanh(mm(band_s[0], xb) + mm(band_s[1], xb))
    act_e = act[:RPAD]
    act_o = act[RPAD:]
    pooled = 0.5 * (act_e + act_o)
    pooled = jnp.where(iota((RPAD, LANES), 0) == ROWS, 1.0, pooled)
    pooled_s = split(pooled)
    rw_only = rws[...]
    rws[ROWS : ROWS + 1, 0:NF] = rb[...]
    rwt_s = split(rws[...].T)
    new_maps = jnp.tanh(mm3(rwt_s, pooled_s))
    fs[0:F, :] = xs[0:F, :]
    fs[F:FT, :] = new_maps[0:NF]
    fg[0:FT, :] = cot[...].astype(f32).reshape(LANES, FT).T
    low = iota((FT, 128), 1) < K
    for m in range(B_DEV // 2):
        pair_s = jnp.concatenate(split(fs[:, 128 * m : 128 * m + 128]), axis=1)
        halves = []
        for s in (2 * m, 2 * m + 1):
            g = gram[s]
            part = mm(g, pair_s) + mm(g, pair_s, TN_DIMS)
            halves.append(part[:, 0:128] + part[:, 128:256])
        fg[0:FT, 128 * m : 128 * m + 128] += jnp.where(low, halves[0], halves[1])
    fg[FT:, :] = jnp.zeros((8, LANES), f32)
    recg = fg[F : F + K, :] * (1.0 - new_maps * new_maps)
    recg = jnp.where(iota((K, LANES), 0) < NF, recg, 0.0)
    recg_s = split(recg)
    half = 0.5 * mm3(split(rw_only), recg_s)
    conv_grad = jnp.concatenate(
        [half * (1.0 - act_e * act_e), half * (1.0 - act_o * act_o)], axis=0
    )
    cg_s = split(conv_grad)
    emb_grad = fg[0:FPAD, :] + mm3(split(band.T), cg_s)
    weight_terms(xb, pooled_s, recg_s, cg_s)

    low = iota((FPAD, 128), 1) < K
    lows, highs = [], []
    for m in range(B_DEV // 2):
        pair = emb_grad[:, 128 * m : 128 * m + 128]
        other = pltpu.roll(pair, K, 1)
        lows += [jnp.where(low, pair, 0.0), jnp.where(low, other, 0.0)]
        highs += [jnp.where(low, 0.0, other), jnp.where(low, 0.0, pair)]
    bag_rows = jnp.concatenate(lows + highs, axis=0).astype(bf16)

    ip[...] = jnp.zeros((B_DEV, 8, 128), i32)
    slot_at = iota((BAG, F), 0)
    for s in range(B_DEV):
        live = slot_at < lengths[s : s + 1, :]
        ip[s, 0:BAG, 0:F] = jnp.where(live, field_table[...] * TROWS + ids[s] + 1, 0)
    value = jnp.zeros((8, 384), i32)
    for s in range(B_DEV):
        wide = jnp.concatenate([ip[s], jnp.zeros((8, 256), i32)], axis=1)
        value = value + (pltpu.roll(wide, FPAD * s, 1) if s else wide)
    value = value[:, 0:BAGS] - 1

    peer_at = jnp.broadcast_to(order[:, 0:1], (N_WIDE, BAGS))
    index_at = iota((N_WIDE, BAGS), 0).astype(f32)
    values, offsets, owned = [], [], []
    count = jnp.zeros((N_WIDE, BAGS), f32)
    for j in range(BAG):
        v = value[j : j + 1, :]
        w = v >> 9
        o = (((w >> 4) - me[0]) & 3) * 16 + (((w >> 1) - me[1]) & 7) * 2 + ((w - me[2]) & 1)
        o = jnp.where(v >= 0, o, -1)
        hit = (peer_at == o).astype(f32)
        values.append(v)
        o = jnp.sum(hit * index_at, axis=0, keepdims=True).astype(i32)
        offsets.append(jnp.where(v >= 0, o, -1))
        owned.append(hit)
        count = count + hit
    before = (iota((BAGS, BAGS), 0) < iota((BAGS, BAGS), 1)).astype(f32).astype(bf16)
    ahead = mm(count.astype(bf16), before)
    near, late = [], []
    codes = jnp.zeros((2 * N_WIDE, 128), f32)
    slot_at = iota((128, BAGS), 0)
    for j in range(BAG):
        rank = jnp.sum(owned[j] * ahead, axis=0, keepdims=True).astype(i32)
        ahead = ahead + owned[j]
        v, o = values[j], offsets[j]
        early = (o >= 0) & (rank < 32)
        after = (o >= 0) & (rank >= 32)
        rest = rank - 32
        near.append(jnp.concatenate(
            [jnp.where(early & ((rank >> 4) == h), o * 16 + (rank & 15), -1) for h in range(2)], axis=1
        ))
        late.append(jnp.concatenate(
            [jnp.where(after & ((rest >> 2) == h), o * 4 + (rest & 3), -1) for h in range(2)], axis=1
        ))
        first = ((v >> 15) * 4 + ((v >> 7) & 3) + 1).astype(f32)
        second = (v & (T_SHARE - 1)).astype(f32)
        lhs = jnp.concatenate([owned[j] * first, owned[j] * second], axis=0).astype(bf16)
        codes = codes + mm(lhs, (slot_at == rank).astype(f32).astype(bf16), NT_DIMS)

    def pick(rows_at, places):
        hit = rows_at == places[0]
        for j in range(1, BAG):
            hit = hit | (rows_at == places[j])
        return mm(hit.astype(f32).astype(bf16), bag_rows)

    stage[...] = jnp.zeros((N_WIDE, 8, 128), f32)
    stage[:, 0:4, :] = pick(iota((256, 2 * BAGS), 0), late).reshape(N_WIDE, 4, 128)
    stage[:, 4, :] = codes[0:N_WIDE] + pltpu.roll(codes[N_WIDE:], K, 1)
    send[:, 16:24, :] = stage[...].astype(bf16)
    for c in range(GROUPS):
        rows = pick(iota((256, 2 * BAGS), 0) + 256 * c, near)
        send[16 * c : 16 * c + 16, 0:16, :] = rows.astype(bf16).reshape(16, 16, 128)


def weight_part(xb, pooled_s, recg_s, cg_s, aux, tz):
    rec_term = mm3(pooled_s, recg_s, NT_DIMS)
    cross = mm(cg_s[0], xb, NT_DIMS) + mm(cg_s[1], xb, NT_DIMS)
    tz[:, 0:FPAD] = cross
    lane = iota((C, 128), 1)
    taps = jnp.zeros((C, 128), f32)
    bias = jnp.zeros((C, 128), f32)
    for p in range(P_SIZE):
        for odd in range(2):
            rows = tz[pl.ds(odd * RPAD + p * C, C), :]
            bias = bias + rows
            taps = taps + pltpu.roll(jnp.where(lane < F, rows, 0.0), (3 - 2 * p - odd) % 128, 1)
    bias = pltpu.roll(jnp.where(lane == F, bias, 0.0), 128 - F + KH, 1)
    taps = jnp.where(lane < KH, taps, 0.0) + bias
    taps = jnp.concatenate([taps, jnp.zeros((128 - C, 128), f32)], axis=0).T[0:8]
    pay = jnp.concatenate([rec_term[0:136], rec_term[136:272]], axis=1)
    aux[:, :, 0, :] = pay[0:64].reshape(8, 8, 128)
    aux[:, :, 1, :] = pay[64:128].reshape(8, 8, 128)
    last = jnp.concatenate([pay[128:136], taps, jnp.zeros((N_WIDE - 16, 128), f32)], axis=0)
    aux[:, :, 2, :] = last.reshape(8, 8, 128)


def windows(codes, first, width):
    n = codes.shape[0]
    lane = iota((n, 128), 1)
    src = iota((n, 128), 0)
    out = pltpu.roll(codes, (128 - first) % 128, 1) if first % 128 else codes
    out = jnp.where(lane < width, out, 0.0)
    by = width
    while by < 128:
        out = out + pltpu.roll(out, by, 1)
        by *= 2
    per = 128 // width
    out = jnp.where(lane // width == (src & (per - 1)), out, 0.0)
    out = jnp.sum(out.reshape(n // per, per, 128), axis=1)
    return jnp.concatenate([out[g : g + 1] for g in range(n // per)], axis=1)


def fill_chunk(vt, g, rows, codes, starts, width):
    turned = rows.T
    row_at = iota((8, 256), 0)
    for h in range(2):
        first = windows(codes, starts[h], width)
        second = windows(codes, 64 + starts[h], width)
        meta = jnp.where(row_at == 0, first, jnp.where(row_at == 1, second, 0.0))
        vt[0, g, h] = jnp.concatenate([turned[K * h : K * h + K], meta], axis=0).astype(bf16)


def add_rows(me_x, vt, acc, slot, g):
    meta = [vt[slot, g, h][K:BLOCK].astype(f32) for h in range(2)]
    rows = jnp.concatenate([vt[slot, g, h][0:K] for h in range(2)], axis=1)
    code = jnp.concatenate([m[0:1] for m in meta], axis=1).astype(i32) - 1
    place = jnp.concatenate([m[1:2] for m in meta], axis=1).astype(i32)
    table_at = code >> 2
    mine = (code >= 0) & ((code & 3) == me_x)
    target = jnp.where(mine, (table_at & 1) * T_SHARE + place, -1)
    hits = (iota((256, 512), 0) == target).astype(f32).astype(bf16)
    pair_at = table_at >> 1
    spread = jnp.concatenate(
        [rows * (pair_at == t).astype(f32).astype(bf16) for t in range(NT // 2)], axis=0
    )
    acc[...] += mm(spread, hits, NT_DIMS)


def whole_kernel(
    cw, cb, emb, cot, gram, rw, rb, ids, lengths, field_table, order,
    acc, red,
    send, stage, es, xs, tz, rws, fs, fg, ip, aux,
    rdat, sums_a, sums_b, part_a, part_b, parts, vt,
    data_sems, send_sems, ring_recv, ring_send, sems,
):
    me_w = lax.axis_index("wide")
    me_x = lax.axis_index("rep")
    right = lax.rem(me_x + 1, N_REP)
    left = lax.rem(me_x + N_REP - 1, N_REP)
    me_line = (me_w // 16) * 2 + lax.rem(me_w, 2)
    me_y, me_z, me_c = me_w // 16, lax.rem(me_w // 2, 8), lax.rem(me_w, 2)

    def on_line(line, z):
        return (line // 2) * 16 + z * 2 + lax.rem(line, 2)

    def wide_copy(src, dst, to, s, r):
        return pltpu.make_async_remote_copy(
            src_ref=src, dst_ref=dst, send_sem=s, recv_sem=r,
            device_id=(to, me_x), device_id_type=MESH,
        )

    def rep_copy(src, dst, to, s, r):
        return pltpu.make_async_remote_copy(
            src_ref=src, dst_ref=dst, send_sem=s, recv_sem=r,
            device_id=(me_w, to), device_id_type=MESH,
        )

    def wait_bytes(ref, n, sem):
        pltpu.make_async_copy(ref.at[pl.ds(0, n)], ref.at[pl.ds(0, n)], sem).wait()

    barrier = pltpu.get_barrier_semaphore()

    def partner(o):
        y, z, c = PARTNERS[o]
        return lax.rem(me_y + y, 4) * 16 + lax.rem(me_z + z, 8) * 2 + lax.rem(me_c + c, 2)

    for o in range(N_WIDE - 1, 0, -1):
        pl.semaphore_signal(
            barrier, inc=1, device_id=(partner(o), me_x), device_id_type=MESH
        )
    for o in range(1, N_REP):
        pl.semaphore_signal(
            barrier, inc=1, device_id=(me_w, lax.rem(me_x + o, N_REP)), device_id_type=MESH
        )

    def others(me, fn):
        def go(o, carry):
            fn(lax.rem(me + o, 8))
            return carry

        lax.fori_loop(1, 8, go, 0)

    dense_part(
        (me_y, me_z, me_c), cw, cb, emb, cot, gram, rw, rb, ids, lengths, field_table, order,
        send, stage, es, xs, tz, rws, fs, fg, ip,
        lambda *terms: weight_part(*terms, aux, tz),
    )
    pl.semaphore_wait(barrier, N_WIDE - 1 + N_REP - 1)
    others(me_line, lambda to: wide_copy(
        aux.at[to], sums_a.at[me_line], on_line(to, me_z), sems.at[0], sems.at[1]
    ).start())
    sums_a[me_line] = aux[me_line]

    for g in ISSUE:
        for o in range(max(1, 16 * g), 16 * g + 16):
            wide_copy(
                send.at[o], rdat.at[o], partner(o), send_sems.at[0], data_sems.at[g]
            ).start()
    wait_bytes(sums_a, 7, sems.at[1])
    part_a[...] = jnp.sum(sums_a[...], axis=0)
    others(me_z, lambda to: wide_copy(
        part_a.at[to], sums_b.at[me_z], on_line(me_line, to), sems.at[2], sems.at[3]
    ).start())
    sums_b[me_z] = part_a[me_z]
    rdat[0] = send[0]
    acc[...] = jnp.zeros(acc.shape, f32)

    def ring(kind, g):
        if kind < 2:
            to, there = ((right, 1), (left, 2))[kind]
            src, dst = vt.at[0, g], vt.at[there, g]
        else:
            slot, h, to = ((1, 0, right), (2, 1, left))[kind - 2]
            src, dst = vt.at[slot, g, h], vt.at[3, g, h]
        return rep_copy(src, dst, to, ring_send.at[kind], ring_recv.at[kind, g])

    def step(g, carry):
        @pl.when(g < GROUPS)
        def _():
            @pl.when(g == 0)
            def _():
                wait_bytes(rdat, 15, data_sems.at[0])

            @pl.when(g > 0)
            def _():
                wait_bytes(rdat, 16, data_sems.at[g])

            got = rdat[pl.ds(16 * g, 16)]
            rows = got[:, 0:16, :].reshape(256, 128).astype(f32)
            codes = got[:, 16:24, :].astype(f32)[:, 4, :]
            fill_chunk(vt, g, rows, codes, (0, 16), 16)

        @pl.when(g == GROUPS)
        def _():
            tail = rdat[:, 16:24, :].astype(f32)
            rows = tail[:, 0:4, :].reshape(256, 128)
            fill_chunk(vt, GROUPS, rows, tail[:, 4, :], (32, 36), 4)

        @pl.when(g < CHUNKS)
        def _():
            for kind in (0, 1):
                ring(kind, g).start()

        @pl.when((g >= ON) & (g < CHUNKS + ON))
        def _():
            ring(0, g - ON).wait_recv()
            ring(2, g - ON).start()
            ring(1, g - ON).wait_recv()
            ring(3, g - ON).start()

        @pl.when(g == AR[0])
        def _():
            wait_bytes(sums_b, 7, sems.at[3])
            part_b[...] = jnp.sum(sums_b[...], axis=0)
            for o in range(1, N_REP):
                to = lax.rem(me_x + o, N_REP)
                rep_copy(part_b, parts.at[me_x], to, sems.at[4], sems.at[5]).start()
            parts[me_x] = part_b[...]

        @pl.when(g == AR[1])
        def _():
            wait_bytes(parts, N_REP - 1, sems.at[5])
            red[me_line, me_z] = (parts[0] + parts[1]) + (parts[2] + parts[3])
            others(me_z, lambda to: wide_copy(
                red.at[me_line, me_z], red.at[me_line, me_z], on_line(me_line, to),
                sems.at[6], sems.at[7],
            ).start())

        @pl.when(g == AR[2])
        def _():
            wait_bytes(sums_b, 7, sems.at[7])
            others(me_line, lambda to: wide_copy(
                red.at[me_line], red.at[me_line], on_line(to, me_z), sems.at[8], sems.at[9]
            ).start())

        @pl.when(g < CHUNKS)
        def _():
            add_rows(me_x, vt, acc, 0, g)

        @pl.when((g >= ON) & (g < CHUNKS + ON))
        def _():
            add_rows(me_x, vt, acc, 1, g - ON)
            add_rows(me_x, vt, acc, 2, g - ON)

        @pl.when(g >= END)
        def _():
            ring(2, g - END).wait_recv()
            ring(3, g - END).wait_recv()
            add_rows(me_x, vt, acc, 3, g - END)

        return carry

    lax.fori_loop(0, CHUNKS + END, step, 0)

    wait_bytes(red, 7, sems.at[9])
    wait_bytes(red, 7, sems.at[8])
    wait_bytes(sums_b, 7, sems.at[6])
    wait_bytes(parts, N_REP - 1, sems.at[4])
    wait_bytes(sums_b, 7, sems.at[2])
    wait_bytes(sums_a, 7, sems.at[0])
    wait_bytes(rdat, N_WIDE - 1, send_sems.at[0])
    for kind in range(4):
        for g in range(CHUNKS):
            ring(kind, g).wait_send()


ISSUE = (0, 1, 2, 3)
AR = (1, 2, 4)
ON = 1
END = 2


def results_kernel(acc, red, table, conv_w, conv_b, rec_w, rec_b, pays, wide_w, sems):
    copies = []
    for t in range(NT):
        half = (t % 2) * T_SHARE
        copies.append(pltpu.make_async_copy(
            acc.at[pl.ds((t // 2) * K, K), pl.ds(half, T_SHARE)], table.at[t], sems.at[t]
        ))
        copies[-1].start()
    scale = 1.0 / math.sqrt(SAMPLES)
    for g in range(3):
        pays[64 * g : 64 * g + 64, :] = red[:, :, g, :].reshape(64, 128) * scale
    wide_w[0:136, :] = pays[0:136, :]
    wide_w[136:272, :] = pltpu.roll(pays[0:136, :], K, 1)
    for p in range(P_SIZE):
        rec_w[p] = wide_w[p * C : (p + 1) * C, 0:NF]
    rec_b[...] = wide_w[ROWS : ROWS + 1, 0:NF]
    conv_w[...] = pays[136 : 136 + KH, 0:C]
    conv_b[...] = pays[136 + KH : 137 + KH, 0:C]
    for copy in copies:
        copy.wait()


def local(
    pooled_emb, conv_weight, conv_bias, rec_weight, rec_bias, feat_cot, gram_cot, bag_ids,
    bag_lengths, field_table,
):
    vmem = pl.BlockSpec(memory_space=pltpu.VMEM)
    order = jnp.asarray([[16 * y + 2 * z + c] * 128 for y, z, c in PARTNERS], i32)
    acc, red = pl.pallas_call(
        whole_kernel,
        out_shape=(
            pltpu.VMEM((NT // 2 * K, 256), f32),
            pltpu.VMEM((8, 8, 3, 128), f32),
        ),
        in_specs=[vmem] * 11,
        out_specs=(vmem,) * 2,
        scratch_shapes=[
            pltpu.VMEM((N_WIDE, MSG, 128), bf16),
            pltpu.VMEM((N_WIDE, 8, 128), f32),
            pltpu.VMEM((F * B_DEV, 128), f32),
            pltpu.VMEM((FPAD, LANES), f32),
            pltpu.VMEM((2 * RPAD, 128), f32),
            pltpu.VMEM((RPAD, K), f32),
            pltpu.VMEM((FT, LANES), f32),
            pltpu.VMEM((FT + 8, LANES), f32),
            pltpu.VMEM((B_DEV, 8, 128), i32),
            pltpu.VMEM((8, 8, 3, 128), f32),
            pltpu.VMEM((N_WIDE, MSG, 128), bf16),
            pltpu.VMEM((8, 8, 3, 128), f32),
            pltpu.VMEM((8, 3, 128), f32),
            pltpu.VMEM((8, 3, 128), f32),
            pltpu.VMEM((3, 128), f32),
            pltpu.VMEM((N_REP, 3, 128), f32),
            pltpu.VMEM((N_REP, CHUNKS, 2, BLOCK, 256), bf16),
            pltpu.SemaphoreType.DMA((GROUPS,)),
            pltpu.SemaphoreType.DMA((1,)),
            pltpu.SemaphoreType.DMA((4, CHUNKS)),
            pltpu.SemaphoreType.DMA((4,)),
            pltpu.SemaphoreType.DMA((10,)),
        ],
        compiler_params=pltpu.CompilerParams(
            vmem_limit_bytes=VMEM_LIMIT, collective_id=0, has_side_effects=True
        ),
        name="whole",
    )(
        conv_weight.T, conv_bias.reshape(1, C), pooled_emb.transpose(1, 0, 2),
        feat_cot.transpose(0, 2, 1), gram_cot, rec_weight.transpose(1, 0, 2),
        rec_bias.reshape(1, NF), bag_ids.transpose(0, 2, 1), bag_lengths,
        field_table.reshape(1, F), order,
    )
    acc = pltpu.with_memory_space_constraint(acc, pltpu.VMEM)
    red = pltpu.with_memory_space_constraint(red, pltpu.VMEM)
    table, conv_w, conv_b, rec_w, rec_b = pl.pallas_call(
        results_kernel,
        out_shape=(
            jax.ShapeDtypeStruct((NT, K, T_SHARE), f32),
            jax.ShapeDtypeStruct((KH, C), f32),
            jax.ShapeDtypeStruct((1, C), f32),
            jax.ShapeDtypeStruct((P_SIZE, C, NF), f32),
            jax.ShapeDtypeStruct((1, NF), f32),
        ),
        in_specs=[vmem] * 2,
        out_specs=(pl.BlockSpec(memory_space=pl.ANY),) + (vmem,) * 4,
        scratch_shapes=[
            pltpu.VMEM((192, 128), f32),
            pltpu.VMEM((RPAD, 128), f32),
            pltpu.SemaphoreType.DMA((NT,)),
        ],
        name="results",
    )(acc, red)
    return table, conv_w.T, conv_b.reshape(C), rec_w.transpose(1, 0, 2), rec_b.reshape(NF)


def solution(mesh):
    in_specs = (
        P(("wide", "rep"), None, None), P(), P(), P(), P(), P(("wide", "rep"), None, None),
        P(("wide", "rep"), None, None), P(("wide", "rep"), None, None), P(("wide", "rep"), None),
        P(),
    )
    out_specs = (P(None, None, ("wide", "rep")), P(), P(), P(), P())
    return jax.shard_map(local, mesh=mesh, in_specs=in_specs, out_specs=out_specs, check_vma=False)
```

```python
import math

import jax
import jax.numpy as jnp
from jax import lax
from jax.experimental import pallas as pl
from jax.experimental.pallas import tpu as pltpu
from jax.sharding import PartitionSpec as P

K = 64
F = 39
NT = 26
C = 14
KH = 7
BAG = 4
B_DEV = 8
T_SHARE = 128
P_SIZE = 19
NF = 57
FT = 96
SAMPLES = 2048
TROWS = 32768
N_WIDE = 64
N_REP = 4

ROWS = C * P_SIZE
RPAD = 272
LANES = B_DEV * K
FPAD = 40
BAGS = B_DEV * FPAD
MSG = 24
PARTNERS = sorted(
    ((y, z, c) for y in range(4) for z in range(8) for c in range(2)),
    key=lambda at: (min(at[0], 4 - at[0]) + min(at[1], 8 - at[1]), at),
)
GROUPS = 4
CHUNKS = GROUPS + 1
BLOCK = 2 * K + 8
MESH = pl.DeviceIdType.MESH
VMEM_LIMIT = 56 * 1024 * 1024
f32 = jnp.float32
bf16 = jnp.bfloat16
i32 = jnp.int32


def split(x):
    hi = x.astype(bf16)
    return hi, (x - hi.astype(f32)).astype(bf16)


def mm(a, b, contract=((1,), (0,))):
    return lax.dot_general(a, b, (contract, ((), ())), preferred_element_type=f32)


def mm3(a, b, contract=((1,), (0,))):
    return mm(a[0], b[0], contract) + (mm(a[1], b[0], contract) + mm(a[0], b[1], contract))


NT_DIMS = ((1,), (1,))
TN_DIMS = ((0,), (0,))


def iota(shape, dim):
    return lax.broadcasted_iota(i32, shape, dim)


def dense_part(
    me, cw, cb, emb, cot, gram, rw, rb, ids, lengths, field_table, order,
    send, stage, es, xs, tz, rws, fs, fg, ip, weight_terms,
):
    es[:, 0:K] = emb[...].astype(f32).reshape(F * B_DEV, K)
    for m in range(B_DEV // 2):
        pair = [es[pl.ds(2 * m + e, F, stride=B_DEV), :][:, 0:K] for e in range(2)]
        xs[0:F, 128 * m : 128 * m + 128] = jnp.concatenate(pair, axis=1)
    xs[F : F + 1, :] = jnp.ones((1, LANES), f32)
    xb = xs[...].astype(bf16)
    taps = jnp.concatenate([cw[...], cb[...]], axis=0).T
    taps = jnp.concatenate([taps, jnp.zeros((C, 120), f32)], axis=1)
    lane = iota((C, 128), 1)
    kernel_taps = jnp.where(lane < KH, taps, 0.0)
    bias_tap = pltpu.roll(jnp.where(lane == KH, taps, 0.0), F - KH, 1)
    tz[ROWS:RPAD, :] = jnp.zeros((RPAD - ROWS, 128), f32)
    tz[RPAD + ROWS :, :] = jnp.zeros((RPAD - ROWS, 128), f32)
    rws[...] = jnp.zeros((RPAD, K), f32)
    for p in range(P_SIZE):
        for odd in range(2):
            moved = pltpu.roll(kernel_taps, (2 * p + odd - 3) % 128, 1)
            rows = pl.ds(odd * RPAD + p * C, C)
            tz[rows, :] = jnp.where(lane < F, moved, 0.0) + bias_tap
        rws[p * C : (p + 1) * C, 0:NF] = rw[p]
    band = tz[:, 0:FPAD]
    band_s = split(band)
    act = jnp.tanh(mm(band_s[0], xb) + mm(band_s[1], xb))
    act_e = act[:RPAD]
    act_o = act[RPAD:]
    pooled = 0.5 * (act_e + act_o)
    pooled = jnp.where(iota((RPAD, LANES), 0) == ROWS, 1.0, pooled)
    pooled_s = split(pooled)
    rw_only = rws[...]
    rws[ROWS : ROWS + 1, 0:NF] = rb[...]
    rwt_s = split(rws[...].T)
    new_maps = jnp.tanh(mm3(rwt_s, pooled_s))
    fs[0:F, :] = xs[0:F, :]
    fs[F:FT, :] = new_maps[0:NF]
    fg[0:FT, :] = cot[...].astype(f32).reshape(LANES, FT).T
    low = iota((FT, 128), 1) < K
    for m in range(B_DEV // 2):
        pair_s = jnp.concatenate(split(fs[:, 128 * m : 128 * m + 128]), axis=1)
        halves = []
        for s in (2 * m, 2 * m + 1):
            g = gram[s]
            part = mm(g, pair_s) + mm(g, pair_s, TN_DIMS)
            halves.append(part[:, 0:128] + part[:, 128:256])
        fg[0:FT, 128 * m : 128 * m + 128] += jnp.where(low, halves[0], halves[1])
    fg[FT:, :] = jnp.zeros((8, LANES), f32)
    recg = fg[F : F + K, :] * (1.0 - new_maps * new_maps)
    recg = jnp.where(iota((K, LANES), 0) < NF, recg, 0.0)
    recg_s = split(recg)
    half = 0.5 * mm3(split(rw_only), recg_s)
    conv_grad = jnp.concatenate(
        [half * (1.0 - act_e * act_e), half * (1.0 - act_o * act_o)], axis=0
    )
    cg_s = split(conv_grad)
    emb_grad = fg[0:FPAD, :] + mm3(split(band.T), cg_s)
    weight_terms(xb, pooled_s, recg_s, cg_s)

    low = iota((FPAD, 128), 1) < K
    lows, highs = [], []
    for m in range(B_DEV // 2):
        pair = emb_grad[:, 128 * m : 128 * m + 128]
        other = pltpu.roll(pair, K, 1)
        lows += [jnp.where(low, pair, 0.0), jnp.where(low, other, 0.0)]
        highs += [jnp.where(low, 0.0, other), jnp.where(low, 0.0, pair)]
    bag_rows = jnp.concatenate(lows + highs, axis=0).astype(bf16)

    ip[...] = jnp.zeros((B_DEV, 8, 128), i32)
    slot_at = iota((BAG, F), 0)
    for s in range(B_DEV):
        live = slot_at < lengths[s : s + 1, :]
        ip[s, 0:BAG, 0:F] = jnp.where(live, field_table[...] * TROWS + ids[s] + 1, 0)
    value = jnp.zeros((8, 384), i32)
    for s in range(B_DEV):
        wide = jnp.concatenate([ip[s], jnp.zeros((8, 256), i32)], axis=1)
        value = value + (pltpu.roll(wide, FPAD * s, 1) if s else wide)
    value = value[:, 0:BAGS] - 1

    peer_at = jnp.broadcast_to(order[:, 0:1], (N_WIDE, BAGS))
    index_at = iota((N_WIDE, BAGS), 0).astype(f32)
    values, offsets, owned = [], [], []
    count = jnp.zeros((N_WIDE, BAGS), f32)
    for j in range(BAG):
        v = value[j : j + 1, :]
        w = v >> 9
        o = (((w >> 4) - me[0]) & 3) * 16 + (((w >> 1) - me[1]) & 7) * 2 + ((w - me[2]) & 1)
        o = jnp.where(v >= 0, o, -1)
        hit = (peer_at == o).astype(f32)
        values.append(v)
        o = jnp.sum(hit * index_at, axis=0, keepdims=True).astype(i32)
        offsets.append(jnp.where(v >= 0, o, -1))
        owned.append(hit)
        count = count + hit
    before = (iota((BAGS, BAGS), 0) < iota((BAGS, BAGS), 1)).astype(f32).astype(bf16)
    ahead = mm(count.astype(bf16), before)
    near, late = [], []
    codes = jnp.zeros((2 * N_WIDE, 128), f32)
    slot_at = iota((128, BAGS), 0)
    for j in range(BAG):
        rank = jnp.sum(owned[j] * ahead, axis=0, keepdims=True).astype(i32)
        ahead = ahead + owned[j]
        v, o = values[j], offsets[j]
        early = (o >= 0) & (rank < 32)
        after = (o >= 0) & (rank >= 32)
        rest = rank - 32
        near.append(jnp.concatenate(
            [jnp.where(early & ((rank >> 4) == h), o * 16 + (rank & 15), -1) for h in range(2)], axis=1
        ))
        late.append(jnp.concatenate(
            [jnp.where(after & ((rest >> 2) == h), o * 4 + (rest & 3), -1) for h in range(2)], axis=1
        ))
        first = ((v >> 15) * 4 + ((v >> 7) & 3) + 1).astype(f32)
        second = (v & (T_SHARE - 1)).astype(f32)
        lhs = jnp.concatenate([owned[j] * first, owned[j] * second], axis=0).astype(bf16)
        codes = codes + mm(lhs, (slot_at == rank).astype(f32).astype(bf16), NT_DIMS)

    def pick(rows_at, places):
        hit = rows_at == places[0]
        for j in range(1, BAG):
            hit = hit | (rows_at == places[j])
        return mm(hit.astype(f32).astype(bf16), bag_rows)

    stage[...] = jnp.zeros((N_WIDE, 8, 128), f32)
    stage[:, 0:4, :] = pick(iota((256, 2 * BAGS), 0), late).reshape(N_WIDE, 4, 128)
    stage[:, 4, :] = codes[0:N_WIDE] + pltpu.roll(codes[N_WIDE:], K, 1)
    send[:, 16:24, :] = stage[...].astype(bf16)
    for c in range(GROUPS):
        rows = pick(iota((256, 2 * BAGS), 0) + 256 * c, near)
        send[16 * c : 16 * c + 16, 0:16, :] = rows.astype(bf16).reshape(16, 16, 128)


def weight_part(xb, pooled_s, recg_s, cg_s, aux, tz):
    rec_term = mm3(pooled_s, recg_s, NT_DIMS)
    cross = mm(cg_s[0], xb, NT_DIMS) + mm(cg_s[1], xb, NT_DIMS)
    tz[:, 0:FPAD] = cross
    lane = iota((C, 128), 1)
    taps = jnp.zeros((C, 128), f32)
    bias = jnp.zeros((C, 128), f32)
    for p in range(P_SIZE):
        for odd in range(2):
            rows = tz[pl.ds(odd * RPAD + p * C, C), :]
            bias = bias + rows
            taps = taps + pltpu.roll(jnp.where(lane < F, rows, 0.0), (3 - 2 * p - odd) % 128, 1)
    bias = pltpu.roll(jnp.where(lane == F, bias, 0.0), 128 - F + KH, 1)
    taps = jnp.where(lane < KH, taps, 0.0) + bias
    taps = jnp.concatenate([taps, jnp.zeros((128 - C, 128), f32)], axis=0).T[0:8]
    pay = jnp.concatenate([rec_term[0:136], rec_term[136:272]], axis=1)
    aux[:, :, 0, :] = pay[0:64].reshape(8, 8, 128)
    aux[:, :, 1, :] = pay[64:128].reshape(8, 8, 128)
    last = jnp.concatenate([pay[128:136], taps, jnp.zeros((N_WIDE - 16, 128), f32)], axis=0)
    aux[:, :, 2, :] = last.reshape(8, 8, 128)


def windows(codes, first, width):
    n = codes.shape[0]
    lane = iota((n, 128), 1)
    src = iota((n, 128), 0)
    out = pltpu.roll(codes, (128 - first) % 128, 1) if first % 128 else codes
    out = jnp.where(lane < width, out, 0.0)
    by = width
    while by < 128:
        out = out + pltpu.roll(out, by, 1)
        by *= 2
    per = 128 // width
    out = jnp.where(lane // width == (src & (per - 1)), out, 0.0)
    out = jnp.sum(out.reshape(n // per, per, 128), axis=1)
    return jnp.concatenate([out[g : g + 1] for g in range(n // per)], axis=1)


def fill_chunk(vt, g, rows, codes, starts, width):
    row_at = iota((8, 256), 0)
    meta = jnp.zeros((8, 256), f32)
    for h in range(2):
        for part in range(2):
            line = windows(codes, 64 * part + starts[h], width)
            meta = jnp.where(row_at == 2 * h + part, line, meta)
    vt[0, g] = jnp.concatenate([rows.T, meta], axis=0).astype(bf16)


def add_rows(me_x, vt, acc, slot, g):
    block = vt[slot, g]
    meta = block[2 * K :].astype(f32)
    rows = jnp.concatenate([block[0:K], block[K : 2 * K]], axis=1)
    code = jnp.concatenate([meta[0:1], meta[2:3]], axis=1).astype(i32) - 1
    place = jnp.concatenate([meta[1:2], meta[3:4]], axis=1).astype(i32)
    table_at = code >> 2
    mine = (code >= 0) & ((code & 3) == me_x)
    target = jnp.where(mine, (table_at & 1) * T_SHARE + place, -1)
    hits = (iota((256, 512), 0) == target).astype(f32).astype(bf16)
    pair_at = table_at >> 1
    spread = jnp.concatenate(
        [rows * (pair_at == t).astype(f32).astype(bf16) for t in range(NT // 2)], axis=0
    )
    acc[...] += mm(spread, hits, NT_DIMS).reshape(acc.shape)


def whole_kernel(
    cw, cb, emb, cot, gram, rw, rb, ids, lengths, field_table, order,
    acc, red,
    send, stage, es, xs, tz, rws, fs, fg, ip, aux,
    rdat, sums_a, sums_b, part_a, part_b, parts, vt,
    data_sems, send_sems, ring_recv, ring_send, sems,
):
    me_w = lax.axis_index("wide")
    me_x = lax.axis_index("rep")
    right = lax.rem(me_x + 1, N_REP)
    left = lax.rem(me_x + N_REP - 1, N_REP)
    me_line = (me_w // 16) * 2 + lax.rem(me_w, 2)
    me_y, me_z, me_c = me_w // 16, lax.rem(me_w // 2, 8), lax.rem(me_w, 2)

    def on_line(line, z):
        return (line // 2) * 16 + z * 2 + lax.rem(line, 2)

    def wide_copy(src, dst, to, s, r):
        return pltpu.make_async_remote_copy(
            src_ref=src, dst_ref=dst, send_sem=s, recv_sem=r,
            device_id=(to, me_x), device_id_type=MESH,
        )

    def rep_copy(src, dst, to, s, r):
        return pltpu.make_async_remote_copy(
            src_ref=src, dst_ref=dst, send_sem=s, recv_sem=r,
            device_id=(me_w, to), device_id_type=MESH,
        )

    def wait_bytes(ref, n, sem):
        pltpu.make_async_copy(ref.at[pl.ds(0, n)], ref.at[pl.ds(0, n)], sem).wait()

    barrier = pltpu.get_barrier_semaphore()

    def partner(o):
        y, z, c = PARTNERS[o]
        return lax.rem(me_y + y, 4) * 16 + lax.rem(me_z + z, 8) * 2 + lax.rem(me_c + c, 2)

    for o in range(N_WIDE - 1, 0, -1):
        pl.semaphore_signal(
            barrier, inc=1, device_id=(partner(o), me_x), device_id_type=MESH
        )
    for o in range(1, N_REP):
        pl.semaphore_signal(
            barrier, inc=1, device_id=(me_w, lax.rem(me_x + o, N_REP)), device_id_type=MESH
        )

    def others(me, fn):
        def go(o, carry):
            fn(lax.rem(me + o, 8))
            return carry

        lax.fori_loop(1, 8, go, 0)

    dense_part(
        (me_y, me_z, me_c), cw, cb, emb, cot, gram, rw, rb, ids, lengths, field_table, order,
        send, stage, es, xs, tz, rws, fs, fg, ip,
        lambda *terms: weight_part(*terms, aux, tz),
    )
    pl.semaphore_wait(barrier, N_WIDE - 1 + N_REP - 1)

    for g in ISSUE:
        for o in range(max(1, 16 * g), 16 * g + 16):
            wide_copy(
                send.at[o], rdat.at[o], partner(o), send_sems.at[0], data_sems.at[g]
            ).start()
    others(me_line, lambda to: wide_copy(
        aux.at[to], sums_a.at[me_line], on_line(to, me_z), sems.at[0], sems.at[1]
    ).start())
    sums_a[me_line] = aux[me_line]
    rdat[0] = send[0]
    acc[...] = jnp.zeros(acc.shape, f32)

    def ring(kind, g):
        if kind < 2:
            to, there = ((right, 1), (left, 2))[kind]
            src, dst = vt.at[0, g], vt.at[there, g]
        else:
            slot, rows, to = ((1, pl.ds(0, K), right), (2, pl.ds(K, BLOCK - K), left))[kind - 2]
            src, dst = vt.at[slot, g, rows], vt.at[3, g, rows]
        return rep_copy(src, dst, to, ring_send.at[kind], ring_recv.at[kind, g])

    def step(g, carry):
        @pl.when(g < GROUPS)
        def _():
            @pl.when(g == 0)
            def _():
                wait_bytes(rdat, 15, data_sems.at[0])

            @pl.when(g > 0)
            def _():
                wait_bytes(rdat, 16, data_sems.at[g])

            got = rdat[pl.ds(16 * g, 16)]
            rows = got[:, 0:16, :].reshape(256, 128).astype(f32)
            codes = got[:, 16:24, :].astype(f32)[:, 4, :]
            fill_chunk(vt, g, rows, codes, (0, 16), 16)

        @pl.when(g < GROUPS)
        def _():
            for kind in (0, 1):
                ring(kind, g).start()

        @pl.when(g == GROUPS - 1)
        def _():
            tail = rdat[:, 16:24, :].astype(f32)
            rows = tail[:, 0:4, :].reshape(256, 128)
            fill_chunk(vt, GROUPS, rows, tail[:, 4, :], (32, 36), 4)
            for kind in (0, 1):
                ring(kind, GROUPS).start()

        @pl.when((g >= ON) & (g < CHUNKS + ON))
        def _():
            ring(0, g - ON).wait_recv()
            ring(2, g - ON).start()
            ring(1, g - ON).wait_recv()
            ring(3, g - ON).start()

        @pl.when(g == AR[3])
        def _():
            wait_bytes(sums_a, 7, sems.at[1])
            part_a[...] = jnp.sum(sums_a[...], axis=0)
            others(me_z, lambda to: wide_copy(
                part_a.at[to], sums_b.at[me_z], on_line(me_line, to), sems.at[2], sems.at[3]
            ).start())
            sums_b[me_z] = part_a[me_z]

        @pl.when(g == AR[0])
        def _():
            wait_bytes(sums_b, 7, sems.at[3])
            part_b[...] = jnp.sum(sums_b[...], axis=0)
            for o in range(1, N_REP):
                to = lax.rem(me_x + o, N_REP)
                rep_copy(part_b, parts.at[me_x], to, sems.at[4], sems.at[5]).start()
            parts[me_x] = part_b[...]

        @pl.when(g == AR[1])
        def _():
            wait_bytes(parts, N_REP - 1, sems.at[5])
            red[me_line, me_z] = (parts[0] + parts[1]) + (parts[2] + parts[3])
            others(me_z, lambda to: wide_copy(
                red.at[me_line, me_z], red.at[me_line, me_z], on_line(me_line, to),
                sems.at[6], sems.at[7],
            ).start())

        @pl.when(g == AR[2])
        def _():
            wait_bytes(sums_b, 7, sems.at[7])
            others(me_line, lambda to: wide_copy(
                red.at[me_line], red.at[me_line], on_line(to, me_z), sems.at[8], sems.at[9]
            ).start())

        @pl.when(g < CHUNKS)
        def _():
            add_rows(me_x, vt, acc, 0, g)

        @pl.when((g >= ON) & (g < CHUNKS + ON))
        def _():
            add_rows(me_x, vt, acc, 1, g - ON)
            add_rows(me_x, vt, acc, 2, g - ON)

        @pl.when(g >= END)
        def _():
            ring(2, g - END).wait_recv()
            ring(3, g - END).wait_recv()
            add_rows(me_x, vt, acc, 3, g - END)

        return carry

    lax.fori_loop(0, CHUNKS + END, step, 0)

    wait_bytes(red, 7, sems.at[9])
    wait_bytes(red, 7, sems.at[8])
    wait_bytes(sums_b, 7, sems.at[6])
    wait_bytes(parts, N_REP - 1, sems.at[4])
    wait_bytes(sums_b, 7, sems.at[2])
    wait_bytes(sums_a, 7, sems.at[0])
    wait_bytes(rdat, N_WIDE - 1, send_sems.at[0])
    for kind in range(4):
        for g in range(CHUNKS):
            ring(kind, g).wait_send()


ISSUE = (0, 1, 3, 2)
AR = (1, 2, 4, 0)
ON = 1
END = 2


def results_kernel(acc, red, table, conv_w, conv_b, rec_w, rec_b, pays, wide_w, sems):
    copies = []
    for half in range(2):
        copies.append(pltpu.make_async_copy(
            acc.at[:, :, pl.ds(half * T_SHARE, T_SHARE)], table.at[:, half], sems.at[half]
        ))
        copies[-1].start()
    scale = 1.0 / math.sqrt(SAMPLES)
    for g in range(3):
        pays[64 * g : 64 * g + 64, :] = red[:, :, g, :].reshape(64, 128) * scale
    wide_w[0:136, :] = pays[0:136, :]
    wide_w[136:272, :] = pltpu.roll(pays[0:136, :], K, 1)
    for p in range(P_SIZE):
        rec_w[p] = wide_w[p * C : (p + 1) * C, 0:NF]
    rec_b[...] = wide_w[ROWS : ROWS + 1, 0:NF]
    conv_w[...] = pays[136 : 136 + KH, 0:C]
    conv_b[...] = pays[136 + KH : 137 + KH, 0:C]
    for copy in copies:
        copy.wait()


def local(
    pooled_emb, conv_weight, conv_bias, rec_weight, rec_bias, feat_cot, gram_cot, bag_ids,
    bag_lengths, field_table,
):
    vmem = pl.BlockSpec(memory_space=pltpu.VMEM)
    order = jnp.asarray([[16 * y + 2 * z + c] * 128 for y, z, c in PARTNERS], i32)
    acc, red = pl.pallas_call(
        whole_kernel,
        out_shape=(
            pltpu.VMEM((NT // 2, K, 256), f32),
            pltpu.VMEM((8, 8, 3, 128), f32),
        ),
        in_specs=[vmem] * 11,
        out_specs=(vmem,) * 2,
        scratch_shapes=[
            pltpu.VMEM((N_WIDE, MSG, 128), bf16),
            pltpu.VMEM((N_WIDE, 8, 128), f32),
            pltpu.VMEM((F * B_DEV, 128), f32),
            pltpu.VMEM((FPAD, LANES), f32),
            pltpu.VMEM((2 * RPAD, 128), f32),
            pltpu.VMEM((RPAD, K), f32),
            pltpu.VMEM((FT, LANES), f32),
            pltpu.VMEM((FT + 8, LANES), f32),
            pltpu.VMEM((B_DEV, 8, 128), i32),
            pltpu.VMEM((8, 8, 3, 128), f32),
            pltpu.VMEM((N_WIDE, MSG, 128), bf16),
            pltpu.VMEM((8, 8, 3, 128), f32),
            pltpu.VMEM((8, 3, 128), f32),
            pltpu.VMEM((8, 3, 128), f32),
            pltpu.VMEM((3, 128), f32),
            pltpu.VMEM((N_REP, 3, 128), f32),
            pltpu.VMEM((N_REP, CHUNKS, BLOCK, 256), bf16),
            pltpu.SemaphoreType.DMA((GROUPS,)),
            pltpu.SemaphoreType.DMA((1,)),
            pltpu.SemaphoreType.DMA((4, CHUNKS)),
            pltpu.SemaphoreType.DMA((4,)),
            pltpu.SemaphoreType.DMA((10,)),
        ],
        compiler_params=pltpu.CompilerParams(
            vmem_limit_bytes=VMEM_LIMIT, collective_id=0, has_side_effects=True
        ),
        name="whole",
    )(
        conv_weight.T, conv_bias.reshape(1, C), pooled_emb.transpose(1, 0, 2),
        feat_cot.transpose(0, 2, 1), gram_cot, rec_weight.transpose(1, 0, 2),
        rec_bias.reshape(1, NF), bag_ids.transpose(0, 2, 1), bag_lengths,
        field_table.reshape(1, F), order,
    )
    acc = pltpu.with_memory_space_constraint(acc, pltpu.VMEM)
    red = pltpu.with_memory_space_constraint(red, pltpu.VMEM)
    table, conv_w, conv_b, rec_w, rec_b = pl.pallas_call(
        results_kernel,
        out_shape=(
            jax.ShapeDtypeStruct((NT // 2, 2, K, T_SHARE), f32),
            jax.ShapeDtypeStruct((KH, C), f32),
            jax.ShapeDtypeStruct((1, C), f32),
            jax.ShapeDtypeStruct((P_SIZE, C, NF), f32),
            jax.ShapeDtypeStruct((1, NF), f32),
        ),
        in_specs=[vmem] * 2,
        out_specs=(pl.BlockSpec(memory_space=pl.ANY),) + (vmem,) * 4,
        scratch_shapes=[
            pltpu.VMEM((192, 128), f32),
            pltpu.VMEM((RPAD, 128), f32),
            pltpu.SemaphoreType.DMA((2,)),
        ],
        name="results",
    )(acc, red)
    table = table.reshape(NT, K, T_SHARE)
    return table, conv_w.T, conv_b.reshape(C), rec_w.transpose(1, 0, 2), rec_b.reshape(NF)


def solution(mesh):
    in_specs = (
        P(("wide", "rep"), None, None), P(), P(), P(), P(), P(("wide", "rep"), None, None),
        P(("wide", "rep"), None, None), P(("wide", "rep"), None, None), P(("wide", "rep"), None),
        P(),
    )
    out_specs = (P(None, None, ("wide", "rep")), P(), P(), P(), P())
    return jax.shard_map(local, mesh=mesh, in_specs=in_specs, out_specs=out_specs, check_vma=False)
```

```python
import math

import jax
import jax.numpy as jnp
from jax import lax
from jax.experimental import pallas as pl
from jax.experimental.pallas import tpu as pltpu
from jax.sharding import PartitionSpec as P

K = 64
F = 39
NT = 26
C = 14
KH = 7
BAG = 4
B_DEV = 8
T_SHARE = 128
P_SIZE = 19
NF = 57
FT = 96
SAMPLES = 2048
TROWS = 32768
N_WIDE = 64
N_REP = 4

ROWS = C * P_SIZE
RPAD = 272
LANES = B_DEV * K
FPAD = 40
BAGS = B_DEV * FPAD
MSG = 24
PARTNERS = sorted(
    ((y, z, c) for y in range(4) for z in range(8) for c in range(2)),
    key=lambda at: (min(at[0], 4 - at[0]) + min(at[1], 8 - at[1]), at),
)
GROUPS = 4
CHUNKS = GROUPS + 1
BLOCK = 2 * K + 8
MESH = pl.DeviceIdType.MESH
VMEM_LIMIT = 56 * 1024 * 1024
f32 = jnp.float32
bf16 = jnp.bfloat16
i32 = jnp.int32


def split(x):
    hi = x.astype(bf16)
    return hi, (x - hi.astype(f32)).astype(bf16)


def mm(a, b, contract=((1,), (0,))):
    return lax.dot_general(a, b, (contract, ((), ())), preferred_element_type=f32)


def mm3(a, b, contract=((1,), (0,))):
    return mm(a[0], b[0], contract) + (mm(a[1], b[0], contract) + mm(a[0], b[1], contract))


NT_DIMS = ((1,), (1,))
TN_DIMS = ((0,), (0,))


def iota(shape, dim):
    return lax.broadcasted_iota(i32, shape, dim)


def dense_part(
    me, cw, cb, emb, cot, gram, rw, rb, ids, lengths, field_table, order,
    send, stage, es, xs, tz, rws, fs, fg, ip, weight_terms,
):
    es[0 : F * B_DEV, 0:K] = emb[...].astype(f32).reshape(F * B_DEV, K)
    for m in range(B_DEV // 2):
        pair = [es[pl.ds(2 * m + e, F, stride=B_DEV), :][:, 0:K] for e in range(2)]
        xs[0:F, 128 * m : 128 * m + 128] = jnp.concatenate(pair, axis=1)
    xs[F : F + 1, :] = jnp.ones((1, LANES), f32)
    xb = xs[...].astype(bf16)
    taps = jnp.concatenate([cw[...], cb[...]], axis=0).T
    taps = jnp.concatenate([taps, jnp.zeros((C, 120), f32)], axis=1)
    lane = iota((C, 128), 1)
    kernel_taps = jnp.where(lane < KH, taps, 0.0)
    bias_tap = pltpu.roll(jnp.where(lane == KH, taps, 0.0), F - KH, 1)
    tz[ROWS:RPAD, :] = jnp.zeros((RPAD - ROWS, 128), f32)
    tz[RPAD + ROWS :, :] = jnp.zeros((RPAD - ROWS, 128), f32)
    rws[...] = jnp.zeros((RPAD, K), f32)
    for p in range(P_SIZE):
        for odd in range(2):
            moved = pltpu.roll(kernel_taps, (2 * p + odd - 3) % 128, 1)
            rows = pl.ds(odd * RPAD + p * C, C)
            tz[rows, :] = jnp.where(lane < F, moved, 0.0) + bias_tap
        rws[p * C : (p + 1) * C, 0:NF] = rw[p]
    band = tz[:, 0:FPAD]
    band_s = split(band)
    act = jnp.tanh(mm(band_s[0], xb) + mm(band_s[1], xb))
    act_e = act[:RPAD]
    act_o = act[RPAD:]
    pooled = 0.5 * (act_e + act_o)
    pooled = jnp.where(iota((RPAD, LANES), 0) == ROWS, 1.0, pooled)
    pooled_s = split(pooled)
    rw_only = rws[...]
    rws[ROWS : ROWS + 1, 0:NF] = rb[...]
    rwt_s = split(rws[...].T)
    new_maps = jnp.tanh(mm3(rwt_s, pooled_s))
    fs[0:F, :] = xs[0:F, :]
    fs[F:FT, :] = new_maps[0:NF]
    fg[0:FT, :] = cot[...].astype(f32).reshape(LANES, FT).T
    low = iota((FT, 128), 1) < K
    for m in range(B_DEV // 2):
        pair_s = jnp.concatenate(split(fs[:, 128 * m : 128 * m + 128]), axis=1)
        halves = []
        for s in (2 * m, 2 * m + 1):
            g = gram[s]
            part = mm(g, pair_s) + mm(g, pair_s, TN_DIMS)
            halves.append(part[:, 0:128] + part[:, 128:256])
        fg[0:FT, 128 * m : 128 * m + 128] += jnp.where(low, halves[0], halves[1])
    fg[FT:, :] = jnp.zeros((8, LANES), f32)
    recg = fg[F : F + K, :] * (1.0 - new_maps * new_maps)
    recg = jnp.where(iota((K, LANES), 0) < NF, recg, 0.0)
    recg_s = split(recg)
    half = 0.5 * mm3(split(rw_only), recg_s)
    conv_grad = jnp.concatenate(
        [half * (1.0 - act_e * act_e), half * (1.0 - act_o * act_o)], axis=0
    )
    cg_s = split(conv_grad)
    emb_grad = fg[0:FPAD, :] + mm3(split(band.T), cg_s)
    weight_terms(xb, pooled_s, recg_s, cg_s)

    low = iota((FPAD, 128), 1) < K
    lows, highs = [], []
    for m in range(B_DEV // 2):
        pair = emb_grad[:, 128 * m : 128 * m + 128]
        other = pltpu.roll(pair, K, 1)
        lows += [jnp.where(low, pair, 0.0), jnp.where(low, other, 0.0)]
        highs += [jnp.where(low, 0.0, other), jnp.where(low, 0.0, pair)]
    bag_rows = jnp.concatenate(lows + highs, axis=0).astype(bf16)

    ip[...] = jnp.zeros((B_DEV, 8, 128), i32)
    slot_at = iota((BAG, F), 0)
    for s in range(B_DEV):
        live = slot_at < lengths[s : s + 1, :]
        ip[s, 0:BAG, 0:F] = jnp.where(live, field_table[...] * TROWS + ids[s] + 1, 0)
    value = jnp.zeros((8, 384), i32)
    for s in range(B_DEV):
        wide = jnp.concatenate([ip[s], jnp.zeros((8, 256), i32)], axis=1)
        value = value + (pltpu.roll(wide, FPAD * s, 1) if s else wide)
    value = value[:, 0:BAGS] - 1

    peer_at = jnp.broadcast_to(order[:, 0:1], (N_WIDE, BAGS))
    index_at = iota((N_WIDE, BAGS), 0).astype(f32)
    values, offsets, owned = [], [], []
    count = jnp.zeros((N_WIDE, BAGS), f32)
    for j in range(BAG):
        v = value[j : j + 1, :]
        w = v >> 9
        o = (((w >> 4) - me[0]) & 3) * 16 + (((w >> 1) - me[1]) & 7) * 2 + ((w - me[2]) & 1)
        o = jnp.where(v >= 0, o, -1)
        hit = (peer_at == o).astype(f32)
        values.append(v)
        o = jnp.sum(hit * index_at, axis=0, keepdims=True).astype(i32)
        offsets.append(jnp.where(v >= 0, o, -1))
        owned.append(hit)
        count = count + hit
    before = (iota((BAGS, BAGS), 0) < iota((BAGS, BAGS), 1)).astype(f32).astype(bf16)
    ahead = mm(count.astype(bf16), before)
    near, late = [], []
    codes = jnp.zeros((2 * N_WIDE, 128), f32)
    slot_at = iota((128, BAGS), 0)
    for j in range(BAG):
        rank = jnp.sum(owned[j] * ahead, axis=0, keepdims=True).astype(i32)
        ahead = ahead + owned[j]
        v, o = values[j], offsets[j]
        early = (o >= 0) & (rank < 32)
        after = (o >= 0) & (rank >= 32)
        rest = rank - 32
        near.append(jnp.concatenate(
            [jnp.where(early & ((rank >> 4) == h), o * 16 + (rank & 15), -1) for h in range(2)], axis=1
        ))
        late.append(jnp.concatenate(
            [jnp.where(after & ((rest >> 2) == h), o * 4 + (rest & 3), -1) for h in range(2)], axis=1
        ))
        first = ((v >> 15) * 4 + ((v >> 7) & 3) + 1).astype(f32)
        second = (v & (T_SHARE - 1)).astype(f32)
        lhs = jnp.concatenate([owned[j] * first, owned[j] * second], axis=0).astype(bf16)
        codes = codes + mm(lhs, (slot_at == rank).astype(f32).astype(bf16), NT_DIMS)

    def pick(rows_at, places):
        hit = rows_at == places[0]
        for j in range(1, BAG):
            hit = hit | (rows_at == places[j])
        return mm(hit.astype(f32).astype(bf16), bag_rows)

    stage[...] = jnp.zeros((N_WIDE, 8, 128), f32)
    stage[:, 0:4, :] = pick(iota((256, 2 * BAGS), 0), late).reshape(N_WIDE, 4, 128)
    stage[:, 4, :] = codes[0:N_WIDE] + pltpu.roll(codes[N_WIDE:], K, 1)
    send[:, 16:24, :] = stage[...].astype(bf16)
    for c in range(GROUPS):
        rows = pick(iota((256, 2 * BAGS), 0) + 256 * c, near)
        send[16 * c : 16 * c + 16, 0:16, :] = rows.astype(bf16).reshape(16, 16, 128)


def weight_part(xb, pooled_s, recg_s, cg_s, aux, tz):
    rec_term = mm3(pooled_s, recg_s, NT_DIMS)
    cross = mm(cg_s[0], xb, NT_DIMS) + mm(cg_s[1], xb, NT_DIMS)
    tz[:, 0:FPAD] = cross
    lane = iota((C, 128), 1)
    taps = jnp.zeros((C, 128), f32)
    bias = jnp.zeros((C, 128), f32)
    for p in range(P_SIZE):
        for odd in range(2):
            rows = tz[pl.ds(odd * RPAD + p * C, C), :]
            bias = bias + rows
            taps = taps + pltpu.roll(jnp.where(lane < F, rows, 0.0), (3 - 2 * p - odd) % 128, 1)
    bias = pltpu.roll(jnp.where(lane == F, bias, 0.0), 128 - F + KH, 1)
    taps = jnp.where(lane < KH, taps, 0.0) + bias
    taps = jnp.concatenate([taps, jnp.zeros((128 - C, 128), f32)], axis=0).T[0:8]
    pay = jnp.concatenate([rec_term[0:136], rec_term[136:272]], axis=1)
    aux[:, :, 0, :] = pay[0:64].reshape(8, 8, 128)
    aux[:, :, 1, :] = pay[64:128].reshape(8, 8, 128)
    last = jnp.concatenate([pay[128:136], taps, jnp.zeros((N_WIDE - 16, 128), f32)], axis=0)
    aux[:, :, 2, :] = last.reshape(8, 8, 128)


def windows(codes, first, width):
    n = codes.shape[0]
    lane = iota((n, 128), 1)
    src = iota((n, 128), 0)
    out = pltpu.roll(codes, (128 - first) % 128, 1) if first % 128 else codes
    out = jnp.where(lane < width, out, 0.0)
    by = width
    while by < 128:
        out = out + pltpu.roll(out, by, 1)
        by *= 2
    per = 128 // width
    out = jnp.where(lane // width == (src & (per - 1)), out, 0.0)
    out = jnp.sum(out.reshape(n // per, per, 128), axis=1)
    return jnp.concatenate([out[g : g + 1] for g in range(n // per)], axis=1)


def fill_chunk(vt, g, rows, codes, starts, width):
    row_at = iota((8, 256), 0)
    meta = jnp.zeros((8, 256), f32)
    for h in range(2):
        for part in range(2):
            line = windows(codes, 64 * part + starts[h], width)
            meta = jnp.where(row_at == 2 * h + part, line, meta)
    vt[0, g] = jnp.concatenate([rows.T, meta], axis=0).astype(bf16)


def add_rows(me_x, vt, acc, slot, g):
    block = vt[slot, g]
    meta = block[2 * K :].astype(f32)
    rows = jnp.concatenate([block[0:K], block[K : 2 * K]], axis=1)
    code = jnp.concatenate([meta[0:1], meta[2:3]], axis=1).astype(i32) - 1
    place = jnp.concatenate([meta[1:2], meta[3:4]], axis=1).astype(i32)
    table_at = code >> 2
    mine = (code >= 0) & ((code & 3) == me_x)
    target = jnp.where(mine, (table_at & 1) * T_SHARE + place, -1)
    hits = (iota((256, 512), 0) == target).astype(f32).astype(bf16)
    pair_at = table_at >> 1
    spread = jnp.concatenate(
        [rows * (pair_at == t).astype(f32).astype(bf16) for t in range(NT // 2)], axis=0
    )
    acc[...] += mm(spread, hits, NT_DIMS).reshape(acc.shape)


def whole_kernel(
    cw, cb, emb, cot, gram, rw, rb, ids, lengths, field_table, order,
    acc, red,
    send, stage, es, xs, tz, rws, fs, fg, ip, aux,
    rdat, sums_a, sums_b, part_a, part_b, parts, vt,
    data_sems, send_sems, ring_recv, ring_send, sems,
):
    me_w = lax.axis_index("wide")
    me_x = lax.axis_index("rep")
    right = lax.rem(me_x + 1, N_REP)
    left = lax.rem(me_x + N_REP - 1, N_REP)
    me_line = (me_w // 16) * 2 + lax.rem(me_w, 2)
    me_y, me_z, me_c = me_w // 16, lax.rem(me_w // 2, 8), lax.rem(me_w, 2)

    def on_line(line, z):
        return (line // 2) * 16 + z * 2 + lax.rem(line, 2)

    def wide_copy(src, dst, to, s, r):
        return pltpu.make_async_remote_copy(
            src_ref=src, dst_ref=dst, send_sem=s, recv_sem=r,
            device_id=(to, me_x), device_id_type=MESH,
        )

    def rep_copy(src, dst, to, s, r):
        return pltpu.make_async_remote_copy(
            src_ref=src, dst_ref=dst, send_sem=s, recv_sem=r,
            device_id=(me_w, to), device_id_type=MESH,
        )

    def wait_bytes(ref, n, sem):
        pltpu.make_async_copy(ref.at[pl.ds(0, n)], ref.at[pl.ds(0, n)], sem).wait()

    barrier = pltpu.get_barrier_semaphore()

    def partner(o):
        y, z, c = PARTNERS[o]
        return lax.rem(me_y + y, 4) * 16 + lax.rem(me_z + z, 8) * 2 + lax.rem(me_c + c, 2)

    for o in range(N_WIDE - 1, 0, -1):
        pl.semaphore_signal(
            barrier, inc=1, device_id=(partner(o), me_x), device_id_type=MESH
        )
    for o in range(1, N_REP):
        pl.semaphore_signal(
            barrier, inc=1, device_id=(me_w, lax.rem(me_x + o, N_REP)), device_id_type=MESH
        )

    def others(me, fn):
        def go(o, carry):
            fn(lax.rem(me + o, 8))
            return carry

        lax.fori_loop(1, 8, go, 0)

    dense_part(
        (me_y, me_z, me_c), cw, cb, emb, cot, gram, rw, rb, ids, lengths, field_table, order,
        send, stage, es, xs, tz, rws, fs, fg, ip,
        lambda *terms: weight_part(*terms, aux, tz),
    )
    pl.semaphore_wait(barrier, N_WIDE - 1 + N_REP - 1)

    for g in ISSUE:
        for o in range(max(1, 16 * g), 16 * g + 16):
            wide_copy(
                send.at[o], rdat.at[o], partner(o), send_sems.at[0], data_sems.at[g]
            ).start()
    others(me_line, lambda to: wide_copy(
        aux.at[to], sums_a.at[me_line], on_line(to, me_z), sems.at[0], sems.at[1]
    ).start())
    sums_a[me_line] = aux[me_line]
    rdat[0] = send[0]
    acc[...] = jnp.zeros(acc.shape, f32)

    def ring(kind, g):
        if kind < 2:
            to, there = ((right, 1), (left, 2))[kind]
            src, dst = vt.at[0, g], vt.at[there, g]
        else:
            slot, rows, to = ((1, pl.ds(0, K), right), (2, pl.ds(K, BLOCK - K), left))[kind - 2]
            src, dst = vt.at[slot, g, rows], vt.at[3, g, rows]
        return rep_copy(src, dst, to, ring_send.at[kind], ring_recv.at[kind, g])

    def step(g, carry):
        @pl.when(g < GROUPS)
        def _():
            @pl.when(g == 0)
            def _():
                wait_bytes(rdat, 15, data_sems.at[0])

            @pl.when(g > 0)
            def _():
                wait_bytes(rdat, 16, data_sems.at[g])

            got = rdat[pl.ds(16 * g, 16)]
            rows = got[:, 0:16, :].reshape(256, 128).astype(f32)
            codes = got[:, 16:24, :].astype(f32)[:, 4, :]
            fill_chunk(vt, g, rows, codes, (0, 16), 16)

        @pl.when(g < GROUPS)
        def _():
            for kind in (0, 1):
                ring(kind, g).start()

        @pl.when(g == GROUPS - 1)
        def _():
            tail = rdat[:, 16:24, :].astype(f32)
            rows = tail[:, 0:4, :].reshape(256, 128)
            fill_chunk(vt, GROUPS, rows, tail[:, 4, :], (32, 36), 4)
            for kind in (0, 1):
                ring(kind, GROUPS).start()

        @pl.when((g >= ON) & (g < CHUNKS + ON))
        def _():
            ring(0, g - ON).wait_recv()
            ring(2, g - ON).start()
            ring(1, g - ON).wait_recv()
            ring(3, g - ON).start()

        @pl.when(g == AR[3])
        def _():
            wait_bytes(sums_a, 7, sems.at[1])
            part_a[...] = jnp.sum(sums_a[...], axis=0)
            others(me_z, lambda to: wide_copy(
                part_a.at[to], sums_b.at[me_z], on_line(me_line, to), sems.at[2], sems.at[3]
            ).start())
            sums_b[me_z] = part_a[me_z]

        @pl.when(g == AR[0])
        def _():
            wait_bytes(sums_b, 7, sems.at[3])
            part_b[...] = jnp.sum(sums_b[...], axis=0)
            for o in range(1, N_REP):
                to = lax.rem(me_x + o, N_REP)
                rep_copy(part_b, parts.at[me_x], to, sems.at[4], sems.at[5]).start()
            parts[me_x] = part_b[...]

        @pl.when(g == AR[1])
        def _():
            wait_bytes(parts, N_REP - 1, sems.at[5])
            red[me_line, me_z] = (parts[0] + parts[1]) + (parts[2] + parts[3])
            others(me_z, lambda to: wide_copy(
                red.at[me_line, me_z], red.at[me_line, me_z], on_line(me_line, to),
                sems.at[6], sems.at[7],
            ).start())

        @pl.when(g == AR[2])
        def _():
            wait_bytes(sums_b, 7, sems.at[7])
            others(me_line, lambda to: wide_copy(
                red.at[me_line], red.at[me_line], on_line(to, me_z), sems.at[8], sems.at[9]
            ).start())

        @pl.when(g < CHUNKS)
        def _():
            add_rows(me_x, vt, acc, 0, g)

        @pl.when((g >= ON) & (g < CHUNKS + ON))
        def _():
            add_rows(me_x, vt, acc, 1, g - ON)
            add_rows(me_x, vt, acc, 2, g - ON)

        @pl.when(g >= END)
        def _():
            ring(2, g - END).wait_recv()
            ring(3, g - END).wait_recv()
            add_rows(me_x, vt, acc, 3, g - END)

        return carry

    lax.fori_loop(0, CHUNKS + END, step, 0)

    wait_bytes(red, 7, sems.at[9])
    wait_bytes(red, 7, sems.at[8])
    wait_bytes(sums_b, 7, sems.at[6])
    wait_bytes(parts, N_REP - 1, sems.at[4])
    wait_bytes(sums_b, 7, sems.at[2])
    wait_bytes(sums_a, 7, sems.at[0])
    wait_bytes(rdat, N_WIDE - 1, send_sems.at[0])
    for kind in range(4):
        for g in range(CHUNKS):
            ring(kind, g).wait_send()


ISSUE = (0, 1, 3, 2)
AR = (1, 2, 4, 0)
ON = 1
END = 2


def results_kernel(acc, red, table, conv_w, conv_b, rec_w, rec_b, pays, wide_w, sems):
    copies = []
    for half in range(2):
        copies.append(pltpu.make_async_copy(
            acc.at[:, :, pl.ds(half * T_SHARE, T_SHARE)], table.at[:, half], sems.at[half]
        ))
        copies[-1].start()
    scale = 1.0 / math.sqrt(SAMPLES)
    for g in range(3):
        pays[64 * g : 64 * g + 64, :] = red[:, :, g, :].reshape(64, 128) * scale
    wide_w[0:136, :] = pays[0:136, :]
    wide_w[136:272, :] = pltpu.roll(pays[0:136, :], K, 1)
    for p in range(P_SIZE):
        rec_w[p] = wide_w[p * C : (p + 1) * C, 0:NF]
    rec_b[...] = wide_w[ROWS : ROWS + 1, 0:NF]
    conv_w[...] = pays[136 : 136 + KH, 0:C]
    conv_b[...] = pays[136 + KH : 137 + KH, 0:C]
    for copy in copies:
        copy.wait()


def local(
    pooled_emb, conv_weight, conv_bias, rec_weight, rec_bias, feat_cot, gram_cot, bag_ids,
    bag_lengths, field_table,
):
    vmem = pl.BlockSpec(memory_space=pltpu.VMEM)
    order = jnp.asarray([[16 * y + 2 * z + c] * 128 for y, z, c in PARTNERS], i32)
    acc, red = pl.pallas_call(
        whole_kernel,
        out_shape=(
            pltpu.VMEM((NT // 2, K, 256), f32),
            pltpu.VMEM((8, 8, 3, 128), f32),
        ),
        in_specs=[vmem] * 11,
        out_specs=(vmem,) * 2,
        scratch_shapes=[
            pltpu.VMEM((N_WIDE, MSG, 128), bf16),
            pltpu.VMEM((N_WIDE, 8, 128), f32),
            pltpu.VMEM((FPAD * B_DEV, 128), f32),
            pltpu.VMEM((FPAD, LANES), f32),
            pltpu.VMEM((2 * RPAD, 128), f32),
            pltpu.VMEM((RPAD, K), f32),
            pltpu.VMEM((FT, LANES), f32),
            pltpu.VMEM((FT + 8, LANES), f32),
            pltpu.VMEM((B_DEV, 8, 128), i32),
            pltpu.VMEM((8, 8, 3, 128), f32),
            pltpu.VMEM((N_WIDE, MSG, 128), bf16),
            pltpu.VMEM((8, 8, 3, 128), f32),
            pltpu.VMEM((8, 3, 128), f32),
            pltpu.VMEM((8, 3, 128), f32),
            pltpu.VMEM((3, 128), f32),
            pltpu.VMEM((N_REP, 3, 128), f32),
            pltpu.VMEM((N_REP, CHUNKS, BLOCK, 256), bf16),
            pltpu.SemaphoreType.DMA((GROUPS,)),
            pltpu.SemaphoreType.DMA((1,)),
            pltpu.SemaphoreType.DMA((4, CHUNKS)),
            pltpu.SemaphoreType.DMA((4,)),
            pltpu.SemaphoreType.DMA((10,)),
        ],
        compiler_params=pltpu.CompilerParams(
            vmem_limit_bytes=VMEM_LIMIT, collective_id=0, has_side_effects=True
        ),
        name="whole",
    )(
        conv_weight.T, conv_bias.reshape(1, C), pooled_emb.transpose(1, 0, 2),
        feat_cot.transpose(0, 2, 1), gram_cot, rec_weight.transpose(1, 0, 2),
        rec_bias.reshape(1, NF), bag_ids.transpose(0, 2, 1), bag_lengths,
        field_table.reshape(1, F), order,
    )
    acc = pltpu.with_memory_space_constraint(acc, pltpu.VMEM)
    red = pltpu.with_memory_space_constraint(red, pltpu.VMEM)
    table, conv_w, conv_b, rec_w, rec_b = pl.pallas_call(
        results_kernel,
        out_shape=(
            jax.ShapeDtypeStruct((NT // 2, 2, K, T_SHARE), f32),
            jax.ShapeDtypeStruct((KH, C), f32),
            jax.ShapeDtypeStruct((1, C), f32),
            jax.ShapeDtypeStruct((P_SIZE, C, NF), f32),
            jax.ShapeDtypeStruct((1, NF), f32),
        ),
        in_specs=[vmem] * 2,
        out_specs=(pl.BlockSpec(memory_space=pl.ANY),) + (vmem,) * 4,
        scratch_shapes=[
            pltpu.VMEM((192, 128), f32),
            pltpu.VMEM((RPAD, 128), f32),
            pltpu.SemaphoreType.DMA((2,)),
        ],
        name="results",
    )(acc, red)
    table = table.reshape(NT, K, T_SHARE)
    return table, conv_w.T, conv_b.reshape(C), rec_w.transpose(1, 0, 2), rec_b.reshape(NF)


def solution(mesh):
    in_specs = (
        P(("wide", "rep"), None, None), P(), P(), P(), P(), P(("wide", "rep"), None, None),
        P(("wide", "rep"), None, None), P(("wide", "rep"), None, None), P(("wide", "rep"), None),
        P(),
    )
    out_specs = (P(None, None, ("wide", "rep")), P(), P(), P(), P())
    return jax.shard_map(local, mesh=mesh, in_specs=in_specs, out_specs=out_specs, check_vma=False)
```
